32 devices in a mesh: seq: 4 (over y, x), head: 8 (over z, core).
Axes of the slice: x: 2, y: 2, z: 4, core: 2. Of those that a mesh axis runs over, the one named last changes fastest.
Arguments:
- q_raw: bfloat16 [1536, 1024], P('seq', 'head'), may hold values from -300 to 300
- k_raw: bfloat16 [1536, 1024], P('seq', 'head'), may hold values from -300 to 300
- values: bfloat16 [1536, 1024], P('seq', 'head'), may hold values from -6 to 6
- out: bfloat16 [1536, 1024], P('seq', 'head'), may hold values from -6 to 6
- d_out: bfloat16 [1536, 1024], P('seq', 'head'), may hold values from -6 to 6
- q_gain: bfloat16 [1024], P('head'), may hold values from 0.25 to 1.75
- k_gain: bfloat16 [1024], P('head'), may hold values from 0.25 to 1.75
- order: int32 [4], replicated, may hold values from 0 to 3, each once
Outputs:
- d_q: bfloat16 [1536, 1024], P('seq', 'head')
- d_k: bfloat16 [1536, 1024], P('seq', 'head')
- d_v: bfloat16 [1536, 1024], P('seq', 'head')
The draws below stay inside these ranges and needn't reach their ends.
All inputs are finite; a program needn't handle non-finite values.
Results may differ from the reference program's by a relative error of at most 0.025.
Values may be sent and summed in bfloat16 or wider, within the bound.
A program may use at most 64 MiB of HBM per device.

```python
import math
import jax
import jax.numpy as jnp
from jax import lax

HEAD_DIM = 128
GROUP = 384
HEADS = 8
TOKENS = 1536
N_SEQ = 4


def apply_scales(key, base, top):
    key_cols, key_rows = jax.random.split(key)
    head_of = jnp.arange(HEADS * HEAD_DIM) // HEAD_DIM
    ramp = jnp.exp(math.log(top) * head_of.astype(jnp.float32) / max(HEADS - 1, 1))
    noise = jnp.exp(jax.random.uniform(key_cols, (HEADS * HEAD_DIM,), jnp.float32, math.log(0.7), math.log(1.4)))
    rows = jnp.exp(jax.random.uniform(key_rows, (TOKENS, 1), jnp.float32, 0.0, math.log(10.0)))
    return (base * ramp[None, :] * noise[None, :] * rows).astype(jnp.bfloat16)


def draw_q_raw(key, part):
    key = jax.random.fold_in(key, 11)
    first, second = jax.random.split(key)
    base = jnp.clip(jax.random.normal(first, (TOKENS, HEADS * HEAD_DIM), jnp.float32), -4.0, 4.0)
    return apply_scales(second, base, 3.0)


def draw_k_raw(key, part):
    key = jax.random.fold_in(key, 12)
    first, second = jax.random.split(key)
    base = jnp.clip(jax.random.normal(first, (TOKENS, HEADS * HEAD_DIM), jnp.float32), -4.0, 4.0)
    return apply_scales(second, base, 1.0 / 3.0)


def shard_levels(stream_key, extent, cuts, low, high):
    def one(dim, shards_of):
        draws = jax.random.uniform(jax.random.fold_in(jax.random.fold_in(stream_key, 6), dim), (shards_of,), jnp.float32, low / len(cuts), high / len(cuts))
        return jnp.repeat(jnp.exp(draws), extent[dim] // shards_of).reshape((-1,) + (1,) * (len(extent) - dim - 1))

    level = one(*cuts[0])
    for cut in cuts[1:]:
        level = level * one(*cut)
    return level


def scatter_about(key, extent, deviation, limit, cuts=(), kind=jnp.bfloat16):
    result = jax.random.normal(key, extent, jnp.float32) * deviation
    if len(cuts) > 0:
        result = shard_levels(key, extent, cuts, -0.22, 0.18) * result
    return jnp.clip(result, min=-limit, max=limit).astype(kind)


def setup_inputs(seed: int = 0) -> dict:
    arg_keys = jax.random.split(jax.random.key(seed), 9)
    return {
        "q_raw": draw_q_raw(jax.random.fold_in(arg_keys[8], 71), 0),
        "k_raw": draw_k_raw(jax.random.fold_in(arg_keys[8], 71), 0),
        "values": scatter_about(arg_keys[2], (TOKENS, HEADS * HEAD_DIM), 1.0, 6.0, ((0, 4), (1, 8))),
        "out": scatter_about(arg_keys[3], (TOKENS, HEADS * HEAD_DIM), 1.0, 6.0, ((0, 4), (1, 8))),
        "d_out": scatter_about(arg_keys[4], (TOKENS, HEADS * HEAD_DIM), 1.0, 6.0, ((0, 4), (1, 8))),
        "q_gain": jnp.clip(1.0 + 0.15 * jax.random.normal(arg_keys[5], (HEADS * HEAD_DIM,), jnp.float32), 0.25, 1.75).astype(jnp.bfloat16),
        "k_gain": jnp.clip(1.0 + 0.15 * jax.random.normal(arg_keys[6], (HEADS * HEAD_DIM,), jnp.float32), 0.25, 1.75).astype(jnp.bfloat16),
        "order": jax.random.permutation(arg_keys[7], N_SEQ).astype(jnp.int32),
    }


EPSILON = 1e-06

def reference(q_raw, k_raw, values, out, d_out, q_gain, k_gain, order):
    feature_count = HEADS * HEAD_DIM
    reciprocal_root = HEAD_DIM ** (-0.5)
    q_float = q_raw.astype(jnp.float32)
    k_float = k_raw.astype(jnp.float32)
    q_rate = lax.rsqrt(lax.optimization_barrier(jnp.mean(q_float * q_float, axis=1)) + EPSILON)
    k_rate = lax.rsqrt(lax.optimization_barrier(jnp.mean(k_float * k_float, axis=1)) + EPSILON)
    q_scale = q_gain.astype(jnp.float32)
    k_scale = k_gain.astype(jnp.float32)
    q_norm = (q_float * q_rate[:, None] * q_scale).astype(jnp.bfloat16)
    k_norm = (k_float * k_rate[:, None] * k_scale).astype(jnp.bfloat16)
    group_of = order[jnp.arange(TOKENS, dtype=jnp.int32) // GROUP]
    visible = group_of[:, None] >= group_of[None, :]

    def one_head(head_index):
        offset = head_index * HEAD_DIM

        def column(array):
            return lax.dynamic_slice_in_dim(array, offset, HEAD_DIM, 1)
        q_head = column(q_norm)
        k_head = column(k_norm)
        v_head = column(values)
        o_head = column(out)
        g_head = column(d_out)
        scores = jnp.dot(q_head, k_head.T, preferred_element_type=jnp.float32) * reciprocal_root
        row_total = lax.optimization_barrier(jnp.sum(jnp.where(visible, jnp.exp(scores), 0.0), axis=1))
        probs = jnp.where(visible, jnp.exp(scores - jnp.log(row_total)[:, None]), 0.0)
        probs_low = probs.astype(jnp.bfloat16)
        delta = lax.optimization_barrier(jnp.sum(g_head.astype(jnp.float32) * o_head.astype(jnp.float32), axis=1))
        dprobs = jnp.dot(g_head, v_head.T, preferred_element_type=jnp.float32)
        dscores = (probs * (dprobs - delta[:, None])).astype(jnp.bfloat16)
        query_grad = jnp.dot(dscores, k_head, preferred_element_type=jnp.float32) * reciprocal_root
        score_grad_tile = dscores.astype(jnp.float32).reshape(N_SEQ, GROUP, TOKENS)
        query_tile = q_head.astype(jnp.float32).reshape(N_SEQ, GROUP, HEAD_DIM)
        key_pieces = (jnp.einsum('faz,fap->fzp', score_grad_tile, query_tile) * reciprocal_root).astype(jnp.bfloat16)
        key_grad = lax.optimization_barrier(jnp.sum(lax.optimization_barrier(key_pieces).astype(jnp.float32), axis=0))
        probability_tile = probs_low.astype(jnp.float32).reshape(N_SEQ, GROUP, TOKENS)
        output_grad_tile = g_head.astype(jnp.float32).reshape(N_SEQ, GROUP, HEAD_DIM)
        value_pieces = jnp.einsum('faz,fap->fzp', probability_tile, output_grad_tile).astype(jnp.bfloat16)
        value_grad = lax.optimization_barrier(jnp.sum(lax.optimization_barrier(value_pieces).astype(jnp.float32), axis=0))
        return (query_grad, key_grad, value_grad)
    query_all, key_all, value_all = lax.map(one_head, jnp.arange(HEADS, dtype=jnp.int32))

    def merge_heads(stacked):
        return jnp.transpose(stacked, (1, 0, 2)).reshape(TOKENS, feature_count)
    q_grad = merge_heads(query_all) * q_scale
    k_grad = merge_heads(key_all) * k_scale
    d_q = q_rate[:, None] * q_grad - q_float * (q_rate ** 3 * lax.optimization_barrier(jnp.sum(q_grad * q_float, axis=1)) / feature_count)[:, None]
    d_k = k_rate[:, None] * k_grad - k_float * (k_rate ** 3 * lax.optimization_barrier(jnp.sum(k_grad * k_float, axis=1)) / feature_count)[:, None]
    return (d_q.astype(jnp.bfloat16), d_k.astype(jnp.bfloat16), merge_heads(value_all).astype(jnp.bfloat16))
```

```python
import functools
import math

import jax
import jax.numpy as jnp
from jax import lax
from jax.experimental import pallas as pl
from jax.experimental.pallas import tpu as pltpu
from jax.sharding import PartitionSpec as P

EPSILON = 1e-06
HIDDEN = -1e30
MESH = pl.DeviceIdType.MESH
NN = (((1,), (0,)), ((), ()))
NT = (((1,), (1,)), ((), ()))


def dot(a, b, dims):
    return lax.dot_general(a, b, dims, preferred_element_type=jnp.float32)


def each(low, high, body):
    if high - low <= 8:
        for j in range(low, high):
            body(j)
    else:

        def step(j, carry):
            body(j)
            return carry

        lax.fori_loop(low, high, step, 0)


def kernel(
    n_s,
    n_h,
    order,
    q_raw,
    k_raw,
    values,
    out,
    d_out,
    q_gain,
    k_gain,
    d_q,
    d_k,
    d_v,
    x_t,
    y_t,
    qg_t,
    kg_t,
    keys,
    keys_t,
    exps,
    dscore,
    maxes,
    dk_sum,
    dv_sum,
    squares,
    grads,
    deltas,
    queries,
    stats,
    dq_out,
    dq_in,
    inner_q,
    inner_k,
    sq_send,
    sq_recv,
    gr_send,
    gr_recv,
    de_send,
    de_recv,
    qu_send,
    qu_recv,
    st_send,
    st_recv,
    dq_send,
    dq_recv,
    iq_send,
    iq_recv,
    ik_send,
    ik_recv,
):
    rows, width = q_raw.shape
    features = n_h * width
    root = width ** (-0.5)
    side = math.isqrt(n_s) if math.isqrt(n_s) ** 2 == n_s else n_s
    tall = n_s // side
    me = lax.axis_index("seq")
    mine = lax.axis_index("head")
    my_y, my_x = lax.div(me, side), lax.rem(me, side)

    def parts(j):
        if isinstance(j, int):
            return j // side, j % side
        return lax.div(j, side), lax.rem(j, side)

    def ahead(j):
        jy, jx = parts(j)
        return lax.rem(my_y + jy, tall) * side + lax.rem(my_x + jx, side)

    def behind(j):
        jy, jx = parts(j)
        return lax.rem(my_y + tall - jy, tall) * side + lax.rem(my_x + side - jx, side)

    def inverse(j):
        jy, jx = parts(j)
        if isinstance(j, int):
            return ((tall - jy) % tall) * side + (side - jx) % side
        return lax.rem(tall - jy, tall) * side + lax.rem(side - jx, side)

    def head_ahead(j):
        return lax.rem(mine + j, n_h)

    def seq_copy(src, dst, send, recv, j, peer):
        return pltpu.make_async_remote_copy(
            src_ref=src,
            dst_ref=dst.at[j],
            send_sem=send.at[j],
            recv_sem=recv.at[j],
            device_id=(peer, mine),
            device_id_type=MESH,
        )

    def head_copy(buffer, send, recv, j):
        return pltpu.make_async_remote_copy(
            src_ref=buffer.at[0],
            dst_ref=buffer.at[j],
            send_sem=send.at[j],
            recv_sem=recv.at[j],
            device_id=(me, head_ahead(j)),
            device_id_type=MESH,
        )

    barrier = pltpu.get_barrier_semaphore()

    def greet_seq(j):
        pl.semaphore_signal(barrier, inc=1, device_id=(ahead(j), mine), device_id_type=MESH)

    def greet_head(j):
        pl.semaphore_signal(barrier, inc=1, device_id=(me, head_ahead(j)), device_id_type=MESH)

    each(1, n_s, greet_seq)
    each(1, n_h, greet_head)

    x = q_raw[...].astype(jnp.float32).T
    y = k_raw[...].astype(jnp.float32).T
    x_t[...] = x
    y_t[...] = y
    squares[0, 0:1] = jnp.sum(x * x, axis=0, keepdims=True)
    squares[0, 1:2] = jnp.sum(y * y, axis=0, keepdims=True)
    grad = d_out[...].astype(jnp.float32)
    grads[0] = grad.T.astype(jnp.bfloat16)
    deltas[0] = jnp.sum((grad * out[...].astype(jnp.float32)).T, axis=0, keepdims=True)
    qg_t[...] = jnp.broadcast_to(q_gain[...].astype(jnp.float32), (rows, width)).T
    kg_t[...] = jnp.broadcast_to(k_gain[...].astype(jnp.float32), (rows, width)).T

    pl.semaphore_wait(barrier, n_s - 1 + n_h - 1)

    def squares_copy(j):
        return head_copy(squares, sq_send, sq_recv, j)

    def grads_copy(j):
        return seq_copy(grads.at[0], grads, gr_send, gr_recv, j, ahead(j))

    def deltas_copy(j):
        return seq_copy(deltas.at[0], deltas, de_send, de_recv, j, ahead(j))

    def queries_copy(j):
        return seq_copy(queries.at[0], queries, qu_send, qu_recv, j, ahead(j))

    def stats_copy(j):
        return seq_copy(stats.at[0], stats, st_send, st_recv, j, ahead(j))

    def dq_copy(j):
        return seq_copy(dq_out.at[j], dq_in, dq_send, dq_recv, j, behind(j))

    def inner_q_copy(j):
        return head_copy(inner_q, iq_send, iq_recv, j)

    def inner_k_copy(j):
        return head_copy(inner_k, ik_send, ik_recv, j)

    each(1, n_h, lambda j: squares_copy(j).start())
    each(1, n_s, lambda j: deltas_copy(j).start())
    each(1, n_s, lambda j: grads_copy(j).start())

    each(1, n_h, lambda j: squares_copy(j).wait_recv())
    rates = lax.rsqrt(jnp.sum(squares[...], axis=0) / features + EPSILON)
    q_rate, k_rate = rates[0:1], rates[1:2]
    queries[0] = (x_t[...] * q_rate * qg_t[...]).astype(jnp.bfloat16)
    each(1, n_s, lambda j: queries_copy(j).start())
    k_norm = y_t[...] * k_rate * kg_t[...]
    keys_t[...] = k_norm.astype(jnp.bfloat16)
    keys[...] = k_norm.T.astype(jnp.bfloat16)
    own_group = order[me]

    def group(j):
        if not (isinstance(j, int) and j == 0):
            grads_copy(j).wait_recv()
            deltas_copy(j).wait_recv()
        dprobs = dot(values[...], grads[j], NN) - deltas[j]
        if not (isinstance(j, int) and j == 0):
            queries_copy(j).wait_recv()
        source = behind(j)
        bias = jnp.where(order[source] >= own_group, 0.0, HIDDEN).astype(jnp.float32)
        scores = dot(keys[...], queries[j], NN) * root
        top = jnp.max(scores, axis=0, keepdims=True)
        probs = jnp.exp(scores - top)
        total = jnp.sum(probs, axis=0, keepdims=True)
        ds = probs * dprobs
        ds_low = ds.astype(jnp.bfloat16)
        exps[j] = probs.astype(jnp.bfloat16)
        dscore[j] = ds_low
        share = 1.0 / total
        moment = jnp.sum(ds * scores, axis=0, keepdims=True) * share
        maxes[j] = top + bias
        stats[0, source, 0:1] = top + bias + jnp.log(total)
        stats[0, source, 1:2] = moment
        dq_out[j] = (dot(keys_t[...], ds_low, NN) * (share * root)).astype(jnp.bfloat16)
        if not (isinstance(j, int) and j == 0):
            dq_copy(j).start()

    group(0)
    each(1, n_s, group)

    each(1, n_s, lambda j: stats_copy(j).start())
    each(1, n_s, lambda j: stats_copy(j).wait_recv())

    def log_total(g):
        logs = [stats[j, g, 0:1] for j in range(n_s)]
        peak = functools.reduce(jnp.maximum, logs)
        return peak + jnp.log(sum(jnp.exp(value - peak) for value in logs))

    own_log = log_total(me)
    weights = [jnp.exp(stats[j, me, 0:1] - own_log) for j in range(n_s)]
    inner_q[0] = sum(weights[j] * stats[j, me, 1:2] for j in range(n_s))
    each(1, n_h, lambda j: inner_q_copy(j).start())

    def key_side(j):
        scale = jnp.exp(maxes[j] - log_total(behind(j)))
        query = (queries[j].astype(jnp.float32) * scale).astype(jnp.bfloat16)
        grad_out = (grads[j].astype(jnp.float32) * scale).astype(jnp.bfloat16)
        dk_add = dot(dscore[j], query, NT)
        dv_add = dot(exps[j], grad_out, NT)
        if isinstance(j, int) and j == 0:
            dk_sum[...] = dk_add
            dv_sum[...] = dv_add
        else:
            dk_sum[...] += dk_add
            dv_sum[...] += dv_add

    key_side(0)
    each(1, n_s, key_side)
    gk = (dk_sum[...] * root).T * kg_t[...]
    inner_k[0] = jnp.sum(gk * y_t[...], axis=0, keepdims=True)
    each(1, n_h, lambda j: inner_k_copy(j).start())
    d_v[...] = dv_sum[...].astype(jnp.bfloat16)

    each(1, n_h, lambda j: inner_q_copy(j).wait_recv())
    each(1, n_h, lambda j: inner_k_copy(j).wait_recv())
    k_total = jnp.sum(inner_k[...], axis=0)
    grad_k = k_rate * gk - y_t[...] * (k_rate * k_rate * k_rate * k_total / features)
    d_k[...] = grad_k.T.astype(jnp.bfloat16)

    q_total = jnp.sum(inner_q[...], axis=0)
    dq = dq_out[0].astype(jnp.float32) * weights[0]
    for j in range(1, n_s):
        dq_copy(j).wait_recv()
        dq = dq + dq_in[j].astype(jnp.float32) * weights[inverse(j)]
    grad_q = q_rate * (dq * qg_t[...]) - x_t[...] * (q_rate * q_rate * q_total / features)
    d_q[...] = grad_q.T.astype(jnp.bfloat16)

    each(1, n_h, lambda j: squares_copy(j).wait_send())
    each(1, n_s, lambda j: grads_copy(j).wait_send())
    each(1, n_s, lambda j: deltas_copy(j).wait_send())
    each(1, n_s, lambda j: queries_copy(j).wait_send())
    each(1, n_s, lambda j: stats_copy(j).wait_send())
    each(1, n_s, lambda j: dq_copy(j).wait_send())
    each(1, n_h, lambda j: inner_q_copy(j).wait_send())
    each(1, n_h, lambda j: inner_k_copy(j).wait_send())


def local(n_s, n_h, q_raw, k_raw, values, out, d_out, q_gain, k_gain, order):
    rows, width = q_raw.shape
    block = jax.ShapeDtypeStruct((rows, width), jnp.bfloat16)
    vmem = pl.BlockSpec(memory_space=pltpu.VMEM)
    smem = pl.BlockSpec(memory_space=pltpu.SMEM)
    low, wide = jnp.bfloat16, jnp.float32
    sems = []
    for count in (n_h, n_s, n_s, n_s, n_s, n_s, n_h, n_h):
        sems += [pltpu.SemaphoreType.DMA((count,))] * 2
    return pl.pallas_call(
        functools.partial(kernel, n_s, n_h),
        out_shape=(block, block, block),
        in_specs=[smem] + [vmem] * 7,
        out_specs=(vmem, vmem, vmem),
        scratch_shapes=[
            pltpu.VMEM((width, rows), wide),
            pltpu.VMEM((width, rows), wide),
            pltpu.VMEM((width, rows), wide),
            pltpu.VMEM((width, rows), wide),
            pltpu.VMEM((rows, width), low),
            pltpu.VMEM((width, rows), low),
            pltpu.VMEM((n_s, rows, rows), low),
            pltpu.VMEM((n_s, rows, rows), low),
            pltpu.VMEM((n_s, 1, rows), wide),
            pltpu.VMEM((rows, width), wide),
            pltpu.VMEM((rows, width), wide),
            pltpu.VMEM((n_h, 2, rows), wide),
            pltpu.VMEM((n_s, width, rows), low),
            pltpu.VMEM((n_s, 1, rows), wide),
            pltpu.VMEM((n_s, width, rows), low),
            pltpu.VMEM((n_s, n_s, 2, rows), wide),
            pltpu.VMEM((n_s, width, rows), low),
            pltpu.VMEM((n_s, width, rows), low),
            pltpu.VMEM((n_h, 1, rows), wide),
            pltpu.VMEM((n_h, 1, rows), wide),
        ]
        + sems,
        compiler_params=pltpu.CompilerParams(
            collective_id=0, has_side_effects=True, vmem_limit_bytes=40 * 1024 * 1024
        ),
        cost_estimate=pl.CostEstimate(
            flops=10 * n_s * rows * rows * width,
            bytes_accessed=16 * rows * width,
            transcendentals=n_s * rows * rows,
        ),
    )(
        order,
        q_raw,
        k_raw,
        values,
        out,
        d_out,
        q_gain.reshape(1, width),
        k_gain.reshape(1, width),
    )


def solution(mesh):
    block = P("seq", "head")
    return jax.shard_map(
        functools.partial(local, mesh.shape["seq"], mesh.shape["head"]),
        mesh=mesh,
        in_specs=(block, block, block, block, block, P("head"), P("head"), P()),
        out_specs=(block, block, block),
        check_vma=False,
    )
```

```python
import functools
import math

import jax
import jax.numpy as jnp
from jax import lax
from jax.experimental import pallas as pl
from jax.experimental.pallas import tpu as pltpu
from jax.sharding import PartitionSpec as P

EPSILON = 1e-06
HIDDEN = -1e30
LOG2E = math.log2(math.e)
MESH = pl.DeviceIdType.MESH
NN = (((1,), (0,)), ((), ()))
NT = (((1,), (1,)), ((), ()))


def dot(a, b, dims):
    return lax.dot_general(a, b, dims, preferred_element_type=jnp.float32)


def each(low, high, body):
    if high - low <= 8:
        for j in range(low, high):
            body(j)
    else:

        def step(j, carry):
            body(j)
            return carry

        lax.fori_loop(low, high, step, 0)


def kernel(
    n_s,
    n_h,
    order_hbm,
    q_hbm,
    k_hbm,
    v_hbm,
    o_hbm,
    do_hbm,
    qg_hbm,
    kg_hbm,
    d_q,
    d_k,
    d_v,
    order,
    q_raw,
    k_raw,
    values,
    out,
    d_out,
    q_gain,
    k_gain,
    x_t,
    y_t,
    qg_t,
    kg_t,
    keys,
    keys_t,
    scores,
    dk_sum,
    dv_sum,
    squares,
    raws,
    queries,
    rows_in,
    grads,
    totals,
    moments,
    dq_out,
    dq_in,
    inner_q,
    inner_k,
    load,
    sq_send,
    sq_recv,
    ra_send,
    ra_recv,
    ro_send,
    ro_recv,
    gr_send,
    gr_recv,
    to_send,
    to_recv,
    mo_send,
    mo_recv,
    dq_send,
    dq_recv,
    iq_send,
    iq_recv,
    ik_send,
    ik_recv,
):
    rows, width = q_raw.shape
    features = n_h * width
    root = width ** (-0.5)
    side = math.isqrt(n_s) if math.isqrt(n_s) ** 2 == n_s else n_s
    tall = n_s // side
    me = lax.axis_index("seq")
    mine = lax.axis_index("head")
    my_y, my_x = lax.div(me, side), lax.rem(me, side)

    def parts(j):
        if isinstance(j, int):
            return j // side, j % side
        return lax.div(j, side), lax.rem(j, side)

    def ahead(j):
        jy, jx = parts(j)
        return lax.rem(my_y + jy, tall) * side + lax.rem(my_x + jx, side)

    def behind(j):
        jy, jx = parts(j)
        return lax.rem(my_y + tall - jy, tall) * side + lax.rem(my_x + side - jx, side)

    def inverse(j):
        jy, jx = parts(j)
        if isinstance(j, int):
            return ((tall - jy) % tall) * side + (side - jx) % side
        return lax.rem(tall - jy, tall) * side + lax.rem(side - jx, side)

    def head_ahead(j):
        return lax.rem(mine + j, n_h)

    def seq_copy(src, dst, send, recv, j, peer):
        return pltpu.make_async_remote_copy(
            src_ref=src,
            dst_ref=dst.at[j],
            send_sem=send.at[j],
            recv_sem=recv.at[j],
            device_id=(peer, mine),
            device_id_type=MESH,
        )

    def head_copy(buffer, send, recv, j):
        return pltpu.make_async_remote_copy(
            src_ref=buffer.at[0],
            dst_ref=buffer.at[j],
            send_sem=send.at[j],
            recv_sem=recv.at[j],
            device_id=(me, head_ahead(j)),
            device_id_type=MESH,
        )

    barrier = pltpu.get_barrier_semaphore()

    def greet_seq(j):
        pl.semaphore_signal(barrier, inc=1, device_id=(ahead(j), mine), device_id_type=MESH)

    def greet_head(j):
        pl.semaphore_signal(barrier, inc=1, device_id=(me, head_ahead(j)), device_id_type=MESH)

    each(1, n_s, greet_seq)
    each(1, n_h, greet_head)

    loads = [
        pltpu.make_async_copy(src, dst, load.at[i])
        for i, (src, dst) in enumerate(
            (
                (q_hbm, q_raw),
                (k_hbm, k_raw),
                (do_hbm, d_out),
                (o_hbm, out),
                (qg_hbm, q_gain),
                (kg_hbm, k_gain),
                (v_hbm, values),
                (order_hbm, order),
            )
        )
    ]
    for copy in loads:
        copy.start()

    loads[0].wait()
    x = q_raw[...].astype(jnp.float32).T
    x_t[...] = x
    raws[0] = x.astype(jnp.bfloat16)
    squares[0, 0:1] = jnp.sum(x * x, axis=0, keepdims=True)
    loads[1].wait()
    y = k_raw[...].astype(jnp.float32).T
    y_t[...] = y
    squares[0, 1:2] = jnp.sum(y * y, axis=0, keepdims=True)

    pl.semaphore_wait(barrier, n_s - 1 + n_h - 1)

    def squares_copy(j):
        return head_copy(squares, sq_send, sq_recv, j)

    def raws_copy(j):
        return seq_copy(raws.at[0], raws, ra_send, ra_recv, j, ahead(j))

    def rows_copy(j):
        return seq_copy(rows_in.at[0], rows_in, ro_send, ro_recv, j, ahead(j))

    def grads_copy(j):
        return seq_copy(grads.at[0], grads, gr_send, gr_recv, j, ahead(j))

    def totals_copy(j):
        return seq_copy(totals.at[0], totals, to_send, to_recv, j, ahead(j))

    def moments_copy(j):
        return seq_copy(moments.at[0, j], moments.at[1], mo_send, mo_recv, j, behind(j))

    def dq_copy(j):
        return seq_copy(dq_out.at[j], dq_in, dq_send, dq_recv, j, behind(j))

    def inner_q_copy(j):
        return head_copy(inner_q, iq_send, iq_recv, j)

    def inner_k_copy(j):
        return head_copy(inner_k, ik_send, ik_recv, j)

    each(1, n_h, lambda j: squares_copy(j).start())
    each(1, n_s, lambda j: raws_copy(j).start())

    loads[2].wait()
    loads[3].wait()
    grad = d_out[...].astype(jnp.float32)
    grads[0] = grad.T.astype(jnp.bfloat16)
    rows_in[0, 1:2] = jnp.sum((grad * out[...].astype(jnp.float32)).T, axis=0, keepdims=True)
    loads[4].wait()
    loads[5].wait()
    qg_t[...] = jnp.broadcast_to(q_gain[...].astype(jnp.float32), (rows, width)).T
    kg_t[...] = jnp.broadcast_to(k_gain[...].astype(jnp.float32), (rows, width)).T

    each(1, n_h, lambda j: squares_copy(j).wait_recv())
    rates = lax.rsqrt(jnp.sum(squares[...], axis=0) / features + EPSILON)
    q_rate, k_rate = rates[0:1], rates[1:2]
    rows_in[0, 0:1] = q_rate
    each(1, n_s, lambda j: rows_copy(j).start())
    each(1, n_s, lambda j: grads_copy(j).start())

    k_norm = y_t[...] * k_rate * kg_t[...]
    keys_t[...] = k_norm.astype(jnp.bfloat16)
    keys[...] = k_norm.T.astype(jnp.bfloat16)
    loads[6].wait()
    loads[7].wait()
    own_group = order[me]

    def hidden(source):
        return jnp.where(order[source] >= own_group, 0.0, HIDDEN).astype(jnp.float32)

    def own(j):
        return isinstance(j, int) and j == 0

    def total_turn(j):
        if not own(j):
            raws_copy(j).wait_recv()
            rows_copy(j).wait_recv()
        query = raws[j].astype(jnp.float32) * rows_in[j, 0:1] * qg_t[...]
        queries[j] = query.astype(jnp.bfloat16)
        source = behind(j)
        score = dot(keys[...], queries[j], NN) * (root * LOG2E) + hidden(source)
        scores[j] = score
        totals[0, source] = jnp.sum(jnp.exp2(score), axis=0, keepdims=True)

    total_turn(0)
    each(1, n_s, total_turn)
    each(1, n_s, lambda j: totals_copy(j).start())
    each(1, n_s, lambda j: totals_copy(j).wait_recv())

    def grad_turn(j):
        if not own(j):
            grads_copy(j).wait_recv()
        source = behind(j)
        log_total = jnp.log2(sum(totals[i, source] for i in range(n_s)))
        score = scores[j]
        probs = jnp.exp2(score - log_total)
        ds = probs * (dot(values[...], grads[j], NN) - rows_in[j, 1:2])
        ds_low = ds.astype(jnp.bfloat16)
        moments[0, j] = jnp.sum(ds * score, axis=0, keepdims=True) * (1.0 / LOG2E)
        if not own(j):
            moments_copy(j).start()
        dq_out[j] = (dot(keys_t[...], ds_low, NN) * root).astype(jnp.bfloat16)
        if not own(j):
            dq_copy(j).start()
        dk_add = dot(ds_low, queries[j], NT)
        dv_add = dot(probs.astype(jnp.bfloat16), grads[j], NT)
        if own(j):
            dk_sum[...] = dk_add
            dv_sum[...] = dv_add
        else:
            dk_sum[...] += dk_add
            dv_sum[...] += dv_add

    grad_turn(0)
    each(1, n_s, grad_turn)

    gk = (dk_sum[...] * root).T * kg_t[...]
    inner_k[0] = jnp.sum(gk * y_t[...], axis=0, keepdims=True)
    each(1, n_h, lambda j: inner_k_copy(j).start())
    each(1, n_s, lambda j: moments_copy(j).wait_recv())
    inner_q[0] = moments[0, 0] + sum(moments[1, j] for j in range(1, n_s))
    each(1, n_h, lambda j: inner_q_copy(j).start())
    d_v[...] = dv_sum[...].astype(jnp.bfloat16)

    each(1, n_h, lambda j: inner_k_copy(j).wait_recv())
    k_total = jnp.sum(inner_k[...], axis=0)
    grad_k = k_rate * gk - y_t[...] * (k_rate * k_rate * k_rate * k_total / features)
    d_k[...] = grad_k.T.astype(jnp.bfloat16)

    dq = dq_out[0].astype(jnp.float32)
    for j in range(1, n_s):
        dq_copy(j).wait_recv()
        dq = dq + dq_in[j].astype(jnp.float32)
    each(1, n_h, lambda j: inner_q_copy(j).wait_recv())
    q_total = jnp.sum(inner_q[...], axis=0)
    grad_q = q_rate * (dq * qg_t[...]) - x_t[...] * (q_rate * q_rate * q_total / features)
    d_q[...] = grad_q.T.astype(jnp.bfloat16)

    each(1, n_h, lambda j: squares_copy(j).wait_send())
    each(1, n_s, lambda j: raws_copy(j).wait_send())
    each(1, n_s, lambda j: rows_copy(j).wait_send())
    each(1, n_s, lambda j: grads_copy(j).wait_send())
    each(1, n_s, lambda j: totals_copy(j).wait_send())
    each(1, n_s, lambda j: moments_copy(j).wait_send())
    each(1, n_s, lambda j: dq_copy(j).wait_send())
    each(1, n_h, lambda j: inner_q_copy(j).wait_send())
    each(1, n_h, lambda j: inner_k_copy(j).wait_send())


def deliver(*refs):
    sems = refs[6]
    copies = [pltpu.make_async_copy(refs[i], refs[i + 3], sems.at[i]) for i in range(3)]
    for copy in copies:
        copy.start()
    for copy in copies:
        copy.wait()


def local(n_s, n_h, q_raw, k_raw, values, out, d_out, q_gain, k_gain, order):
    rows, width = q_raw.shape
    block = jax.ShapeDtypeStruct((rows, width), jnp.bfloat16)
    vmem = pl.BlockSpec(memory_space=pltpu.VMEM)
    hbm = pl.BlockSpec(memory_space=pltpu.HBM)
    low, wide = jnp.bfloat16, jnp.float32
    sems = [pltpu.SemaphoreType.DMA((8,))]
    for count in (n_h, n_s, n_s, n_s, n_s, n_s, n_s, n_h, n_h):
        sems += [pltpu.SemaphoreType.DMA((count,))] * 2
    results = pl.pallas_call(
        functools.partial(kernel, n_s, n_h),
        out_shape=(block, block, block),
        in_specs=[hbm] * 8,
        out_specs=(vmem, vmem, vmem),
        scratch_shapes=[
            pltpu.SMEM((n_s,), jnp.int32),
            pltpu.VMEM((rows, width), low),
            pltpu.VMEM((rows, width), low),
            pltpu.VMEM((rows, width), low),
            pltpu.VMEM((rows, width), low),
            pltpu.VMEM((rows, width), low),
            pltpu.VMEM((1, width), low),
            pltpu.VMEM((1, width), low),
            pltpu.VMEM((width, rows), wide),
            pltpu.VMEM((width, rows), wide),
            pltpu.VMEM((width, rows), wide),
            pltpu.VMEM((width, rows), wide),
            pltpu.VMEM((rows, width), low),
            pltpu.VMEM((width, rows), low),
            pltpu.VMEM((n_s, rows, rows), wide),
            pltpu.VMEM((rows, width), wide),
            pltpu.VMEM((rows, width), wide),
            pltpu.VMEM((n_h, 2, rows), wide),
            pltpu.VMEM((n_s, width, rows), low),
            pltpu.VMEM((n_s, width, rows), low),
            pltpu.VMEM((n_s, 2, rows), wide),
            pltpu.VMEM((n_s, width, rows), low),
            pltpu.VMEM((n_s, n_s, 1, rows), wide),
            pltpu.VMEM((2, n_s, 1, rows), wide),
            pltpu.VMEM((n_s, width, rows), low),
            pltpu.VMEM((n_s, width, rows), low),
            pltpu.VMEM((n_h, 1, rows), wide),
            pltpu.VMEM((n_h, 1, rows), wide),
        ]
        + sems,
        compiler_params=pltpu.CompilerParams(
            collective_id=0, has_side_effects=True, vmem_limit_bytes=40 * 1024 * 1024
        ),
        cost_estimate=pl.CostEstimate(
            flops=10 * n_s * rows * rows * width,
            bytes_accessed=16 * rows * width,
            transcendentals=2 * n_s * rows * rows,
        ),
    )(
        *(
            pltpu.with_memory_space_constraint(array, pltpu.HBM)
            for array in (
                order,
                q_raw,
                k_raw,
                values,
                out,
                d_out,
                q_gain.reshape(1, width),
                k_gain.reshape(1, width),
            )
        )
    )
    return pl.pallas_call(
        deliver,
        out_shape=(block, block, block),
        in_specs=[vmem] * 3,
        out_specs=(hbm, hbm, hbm),
        scratch_shapes=[pltpu.SemaphoreType.DMA((3,))],
    )(*results)


def solution(mesh):
    block = P("seq", "head")
    return jax.shard_map(
        functools.partial(local, mesh.shape["seq"], mesh.shape["head"]),
        mesh=mesh,
        in_specs=(block, block, block, block, block, P("head"), P("head"), P()),
        out_specs=(block, block, block),
        check_vma=False,
    )
```

```python
import functools
import math

import jax
import jax.numpy as jnp
from jax import lax
from jax.experimental import pallas as pl
from jax.experimental.pallas import tpu as pltpu
from jax.sharding import PartitionSpec as P

EPSILON = 1e-06
HIDDEN = -1e30
LOG2E = math.log2(math.e)
MESH = pl.DeviceIdType.MESH
NN = (((1,), (0,)), ((), ()))
NT = (((1,), (1,)), ((), ()))


def dot(a, b, dims):
    return lax.dot_general(a, b, dims, preferred_element_type=jnp.float32)


def each(low, high, body):
    if high - low <= 8:
        for j in range(low, high):
            body(j)
    else:

        def step(j, carry):
            body(j)
            return carry

        lax.fori_loop(low, high, step, 0)


def grid_of(n_s):
    root = math.isqrt(n_s)
    return (root, root) if root * root == n_s else (n_s, 1)


def kernel(
    n_s,
    n_h,
    order_hbm,
    q_hbm,
    k_hbm,
    v_hbm,
    o_hbm,
    do_hbm,
    qg_hbm,
    kg_hbm,
    d_q,
    d_k,
    d_v,
    order,
    q_raw,
    k_raw,
    out,
    d_out,
    q_gain,
    k_gain,
    x_t,
    q_scale,
    k_scale,
    qg_t,
    kg_t,
    keys,
    keys_t,
    queries,
    scores,
    squares,
    q_in,
    k_in,
    q_rows,
    k_rows,
    grads,
    values,
    totals,
    q_moment,
    k_moment,
    dq_out,
    dq_in,
    dk_out,
    dk_in,
    dv_out,
    dv_in,
    inner,
    load,
    sq_send,
    sq_recv,
    qi_send,
    qi_recv,
    ki_send,
    ki_recv,
    qr_send,
    qr_recv,
    kr_send,
    kr_recv,
    gr_send,
    gr_recv,
    va_send,
    va_recv,
    to_send,
    to_recv,
    qm_send,
    qm_recv,
    km_send,
    km_recv,
    dq_send,
    dq_recv,
    dk_send,
    dk_recv,
    dv_send,
    dv_recv,
    inn_send,
    inn_recv,
):
    rows, width = q_raw.shape
    features = n_h * width
    root = width ** (-0.5)
    side, tall = grid_of(n_s)
    me = lax.axis_index("seq")
    mine = lax.axis_index("head")
    my_y, my_x = lax.div(me, side), lax.rem(me, side)

    def row_peer(step):
        return my_y * side + lax.rem(my_x + step, side)

    def column_peer(step):
        return lax.rem(my_y + step, tall) * side + my_x

    def head_peer(step):
        return lax.rem(mine + step, n_h)

    def remote(src, dst, send, recv, j, seq, head):
        return pltpu.make_async_remote_copy(
            src_ref=src,
            dst_ref=dst,
            send_sem=send.at[j],
            recv_sem=recv.at[j],
            device_id=(seq, head),
            device_id_type=MESH,
        )

    def to_row(buffer, send, recv):
        return lambda j: remote(
            buffer.at[0], buffer.at[j], send, recv, j, row_peer(j), mine
        )

    def to_column(buffer, send, recv):
        return lambda j: remote(
            buffer.at[0], buffer.at[j], send, recv, j, column_peer(j), mine
        )

    def to_heads(buffer, send, recv):
        return lambda j: remote(buffer.at[0], buffer.at[j], send, recv, j, me, head_peer(j))

    def back_row(source, target, send, recv):
        return lambda j: remote(
            source.at[j], target.at[j], send, recv, j, row_peer(side - j), mine
        )

    def back_column(source, target, send, recv):
        return lambda j: remote(
            source.at[j], target.at[j], send, recv, j, column_peer(tall - j), mine
        )

    barrier = pltpu.get_barrier_semaphore()

    def greet(seq, head):
        pl.semaphore_signal(barrier, inc=1, device_id=(seq, head), device_id_type=MESH)

    each(1, side, lambda j: greet(row_peer(j), mine))
    each(1, tall, lambda j: greet(column_peer(j), mine))
    each(1, n_h, lambda j: greet(me, head_peer(j)))

    loads = [
        pltpu.make_async_copy(src, dst, load.at[i])
        for i, (src, dst) in enumerate(
            (
                (q_hbm, q_raw),
                (k_hbm, k_raw),
                (do_hbm, d_out),
                (o_hbm, out),
                (qg_hbm, q_gain),
                (kg_hbm, k_gain),
                (v_hbm, values.at[0]),
                (order_hbm, order),
            )
        )
    ]
    for copy in loads:
        copy.start()

    squares_copy = to_heads(squares, sq_send, sq_recv)
    q_copy = to_row(q_in, qi_send, qi_recv)
    k_copy = to_column(k_in, ki_send, ki_recv)
    q_rows_copy = to_row(q_rows, qr_send, qr_recv)
    k_rows_copy = to_column(k_rows, kr_send, kr_recv)
    grads_copy = to_row(grads, gr_send, gr_recv)
    values_copy = to_column(values, va_send, va_recv)
    totals_copy = to_row(totals, to_send, to_recv)
    q_moment_copy = back_row(q_moment.at[0], q_moment.at[1], qm_send, qm_recv)
    k_moment_copy = back_column(k_moment.at[0], k_moment.at[1], km_send, km_recv)
    dq_copy = back_row(dq_out, dq_in, dq_send, dq_recv)
    dk_copy = back_column(dk_out, dk_in, dk_send, dk_recv)
    dv_copy = back_column(dv_out, dv_in, dv_send, dv_recv)
    inner_copy = to_heads(inner, inn_send, inn_recv)

    loads[0].wait()
    x = q_raw[...].astype(jnp.float32).T
    x_t[...] = x
    q_in[0] = x.astype(jnp.bfloat16)
    squares[0, 0:1] = jnp.sum(x * x, axis=0, keepdims=True)
    loads[1].wait()
    y = k_raw[...].astype(jnp.float32).T
    k_in[0] = y.astype(jnp.bfloat16)
    squares[0, 1:2] = jnp.sum(y * y, axis=0, keepdims=True)

    pl.semaphore_wait(barrier, side + tall + n_h - 3)
    each(1, n_h, lambda j: squares_copy(j).start())
    each(1, side, lambda j: q_copy(j).start())
    each(1, tall, lambda j: k_copy(j).start())

    loads[2].wait()
    loads[3].wait()
    grad = d_out[...].astype(jnp.float32)
    grads[0] = grad.T.astype(jnp.bfloat16)
    q_rows[0, 1:2] = jnp.sum((grad * out[...].astype(jnp.float32)).T, axis=0, keepdims=True)
    loads[4].wait()
    loads[5].wait()
    qg_t[...] = jnp.broadcast_to(q_gain[...].astype(jnp.float32), (rows, width)).T
    kg_t[...] = jnp.broadcast_to(k_gain[...].astype(jnp.float32), (rows, width)).T
    loads[6].wait()
    loads[7].wait()

    each(1, n_h, lambda j: squares_copy(j).wait_recv())
    rates = lax.rsqrt(jnp.sum(squares[...], axis=0) / features + EPSILON)
    q_rate, k_rate = rates[0:1], rates[1:2]
    q_rows[0, 0:1] = q_rate
    k_rows[0] = k_rate
    each(1, side, lambda j: q_rows_copy(j).start())
    each(1, tall, lambda j: k_rows_copy(j).start())
    each(1, side, lambda j: grads_copy(j).start())
    each(1, tall, lambda j: values_copy(j).start())

    def form_query(j):
        query = q_in[j].astype(jnp.float32) * q_rows[j, 0:1] * qg_t[...]
        queries[j] = query.astype(jnp.bfloat16)

    def form_keys(j):
        key = k_in[j].astype(jnp.float32) * k_rows[j] * kg_t[...]
        keys_t[j] = key.astype(jnp.bfloat16)
        keys[j] = key.T.astype(jnp.bfloat16)

    row_total = [0.0] * side

    def score_tile(jx, jy):
        query_group = order[row_peer(side - jx)]
        key_group = order[column_peer(tall - jy)]
        hidden = jnp.where(query_group >= key_group, 0.0, HIDDEN).astype(jnp.float32)
        score = dot(keys[jy], queries[jx], NN) * (root * LOG2E) + hidden
        scores[jx, jy] = score
        row_total[jx] += jnp.sum(jnp.exp2(score), axis=0, keepdims=True)

    form_query(0)
    form_keys(0)
    score_tile(0, 0)
    for jx in range(1, side):
        q_copy(jx).wait_recv()
        q_rows_copy(jx).wait_recv()
        form_query(jx)
        score_tile(jx, 0)
    for jy in range(1, tall):
        k_copy(jy).wait_recv()
        k_rows_copy(jy).wait_recv()
        form_keys(jy)
        for jx in range(side):
            score_tile(jx, jy)
    for jx in range(side):
        totals[0, lax.rem(my_x + side - jx, side)] = row_total[jx]
    each(1, side, lambda j: totals_copy(j).start())
    q_scale[...] = q_rate * qg_t[...]
    k_scale[...] = (k_rate * kg_t[...]).T
    each(1, side, lambda j: totals_copy(j).wait_recv())

    logs = [
        jnp.log2(sum(totals[i, lax.rem(my_x + side - jx, side)] for i in range(side)))
        for jx in range(side)
    ]
    ones = jnp.ones((16, rows), jnp.bfloat16)
    dq = [0.0] * side
    dk = [0.0] * tall
    dv = [0.0] * tall
    q_part = [0.0] * side
    k_part = [0.0] * tall

    def grad_tile(jx, jy):
        score = scores[jx, jy]
        probs = jnp.exp2(score - logs[jx])
        ds = probs * (dot(values[jy], grads[jx], NN) - q_rows[jx, 1:2])
        low = ds.astype(jnp.bfloat16)
        moment = ds * score
        q_part[jx] += jnp.sum(moment, axis=0, keepdims=True)
        k_part[jy] += dot(ones, moment.astype(jnp.bfloat16), NT)[0:1]
        dq[jx] += dot(keys_t[jy], low, NN)
        dk[jy] += dot(low, queries[jx], NT)
        dv[jy] += dot(probs.astype(jnp.bfloat16), grads[jx], NT)

    grad_tile(0, 0)
    for jx in range(1, side):
        grads_copy(jx).wait_recv()
    for jy in range(1, tall):
        values_copy(jy).wait_recv()
        for jx in range(side):
            grad_tile(jx, jy)
        k_moment[0, jy] = k_part[jy]
        k_moment_copy(jy).start()
        dk_out[jy] = (dk[jy] * root).astype(jnp.bfloat16)
        dk_copy(jy).start()
        dv_out[jy] = dv[jy].astype(jnp.bfloat16)
        dv_copy(jy).start()
    for jx in range(1, side):
        grad_tile(jx, 0)
        q_moment[0, jx] = q_part[jx]
        q_moment_copy(jx).start()
        dq_out[jx] = (dq[jx] * root).astype(jnp.bfloat16)
        dq_copy(jx).start()

    q_inner, k_inner = q_part[0], k_part[0]
    for jy in range(1, tall):
        k_moment_copy(jy).wait_recv()
        k_inner = k_inner + k_moment[1, jy]
    for jx in range(1, side):
        q_moment_copy(jx).wait_recv()
        q_inner = q_inner + q_moment[1, jx]
    inner[0, 0:1] = q_inner
    inner[0, 1:2] = k_inner
    each(1, n_h, lambda j: inner_copy(j).start())

    own_dq = dq[0] * root
    own_dk = dk[0] * root
    each(1, n_h, lambda j: inner_copy(j).wait_recv())
    products = jnp.sum(inner[...], axis=0) * (1.0 / (LOG2E * features))
    for jx in range(1, side):
        dq_copy(jx).wait_recv()
        own_dq = own_dq + dq_in[jx].astype(jnp.float32)
    grad_q = q_scale[...] * own_dq - x_t[...] * (q_rate * q_rate * products[0:1])
    d_q[...] = grad_q.T.astype(jnp.bfloat16)
    for jy in range(1, tall):
        dk_copy(jy).wait_recv()
        own_dk = own_dk + dk_in[jy].astype(jnp.float32)
    pull = jnp.broadcast_to(k_rate * k_rate * products[1:2], (width, rows)).T
    d_k[...] = (k_scale[...] * own_dk - k_raw[...].astype(jnp.float32) * pull).astype(jnp.bfloat16)
    own_dv = dv[0]
    for jy in range(1, tall):
        dv_copy(jy).wait_recv()
        own_dv = own_dv + dv_in[jy].astype(jnp.float32)
    d_v[...] = own_dv.astype(jnp.bfloat16)

    for copy in (squares_copy, inner_copy):
        each(1, n_h, lambda j: copy(j).wait_send())
    for copy in (q_copy, q_rows_copy, grads_copy, totals_copy, q_moment_copy, dq_copy):
        each(1, side, lambda j: copy(j).wait_send())
    for copy in (k_copy, k_rows_copy, values_copy, k_moment_copy, dk_copy, dv_copy):
        each(1, tall, lambda j: copy(j).wait_send())


def deliver(*refs):
    sems = refs[6]
    copies = [pltpu.make_async_copy(refs[i], refs[i + 3], sems.at[i]) for i in range(3)]
    for copy in copies:
        copy.start()
    for copy in copies:
        copy.wait()


def local(n_s, n_h, q_raw, k_raw, values, out, d_out, q_gain, k_gain, order):
    rows, width = q_raw.shape
    block = jax.ShapeDtypeStruct((rows, width), jnp.bfloat16)
    vmem = pl.BlockSpec(memory_space=pltpu.VMEM)
    hbm = pl.BlockSpec(memory_space=pltpu.HBM)
    low, wide = jnp.bfloat16, jnp.float32
    side, tall = grid_of(n_s)
    results = pl.pallas_call(
        functools.partial(kernel, n_s, n_h),
        out_shape=(block, block, block),
        in_specs=[hbm] * 8,
        out_specs=(vmem, vmem, vmem),
        scratch_shapes=[
            pltpu.SMEM((n_s,), jnp.int32),
            pltpu.VMEM((rows, width), low),
            pltpu.VMEM((rows, width), low),
            pltpu.VMEM((rows, width), low),
            pltpu.VMEM((rows, width), low),
            pltpu.VMEM((1, width), low),
            pltpu.VMEM((1, width), low),
            pltpu.VMEM((width, rows), wide),
            pltpu.VMEM((width, rows), wide),
            pltpu.VMEM((rows, width), wide),
            pltpu.VMEM((width, rows), wide),
            pltpu.VMEM((width, rows), wide),
            pltpu.VMEM((tall, rows, width), low),
            pltpu.VMEM((tall, width, rows), low),
            pltpu.VMEM((side, width, rows), low),
            pltpu.VMEM((side, tall, rows, rows), wide),
            pltpu.VMEM((n_h, 2, rows), wide),
            pltpu.VMEM((side, width, rows), low),
            pltpu.VMEM((tall, width, rows), low),
            pltpu.VMEM((side, 2, rows), wide),
            pltpu.VMEM((tall, 1, rows), wide),
            pltpu.VMEM((side, width, rows), low),
            pltpu.VMEM((tall, rows, width), low),
            pltpu.VMEM((side, side, 1, rows), wide),
            pltpu.VMEM((2, side, 1, rows), wide),
            pltpu.VMEM((2, tall, 1, rows), wide),
            pltpu.VMEM((side, width, rows), low),
            pltpu.VMEM((side, width, rows), low),
            pltpu.VMEM((tall, rows, width), low),
            pltpu.VMEM((tall, rows, width), low),
            pltpu.VMEM((tall, rows, width), low),
            pltpu.VMEM((tall, rows, width), low),
            pltpu.VMEM((n_h, 2, rows), wide),
            pltpu.SemaphoreType.DMA((8,)),
            pltpu.SemaphoreType.DMA((n_h,)),
            pltpu.SemaphoreType.DMA((n_h,)),
            pltpu.SemaphoreType.DMA((side,)),
            pltpu.SemaphoreType.DMA((side,)),
            pltpu.SemaphoreType.DMA((tall,)),
            pltpu.SemaphoreType.DMA((tall,)),
            pltpu.SemaphoreType.DMA((side,)),
            pltpu.SemaphoreType.DMA((side,)),
            pltpu.SemaphoreType.DMA((tall,)),
            pltpu.SemaphoreType.DMA((tall,)),
            pltpu.SemaphoreType.DMA((side,)),
            pltpu.SemaphoreType.DMA((side,)),
            pltpu.SemaphoreType.DMA((tall,)),
            pltpu.SemaphoreType.DMA((tall,)),
            pltpu.SemaphoreType.DMA((side,)),
            pltpu.SemaphoreType.DMA((side,)),
            pltpu.SemaphoreType.DMA((side,)),
            pltpu.SemaphoreType.DMA((side,)),
            pltpu.SemaphoreType.DMA((tall,)),
            pltpu.SemaphoreType.DMA((tall,)),
            pltpu.SemaphoreType.DMA((side,)),
            pltpu.SemaphoreType.DMA((side,)),
            pltpu.SemaphoreType.DMA((tall,)),
            pltpu.SemaphoreType.DMA((tall,)),
            pltpu.SemaphoreType.DMA((tall,)),
            pltpu.SemaphoreType.DMA((tall,)),
            pltpu.SemaphoreType.DMA((n_h,)),
            pltpu.SemaphoreType.DMA((n_h,)),
        ],
        compiler_params=pltpu.CompilerParams(
            collective_id=0, has_side_effects=True, vmem_limit_bytes=40 * 1024 * 1024
        ),
        cost_estimate=pl.CostEstimate(
            flops=10 * n_s * rows * rows * width,
            bytes_accessed=16 * rows * width,
            transcendentals=2 * n_s * rows * rows,
        ),
    )(
        *(
            pltpu.with_memory_space_constraint(array, pltpu.HBM)
            for array in (
                order,
                q_raw,
                k_raw,
                values,
                out,
                d_out,
                q_gain.reshape(1, width),
                k_gain.reshape(1, width),
            )
        )
    )
    return pl.pallas_call(
        deliver,
        out_shape=(block, block, block),
        in_specs=[vmem] * 3,
        out_specs=(hbm, hbm, hbm),
        scratch_shapes=[pltpu.SemaphoreType.DMA((3,))],
        compiler_params=pltpu.CompilerParams(vmem_limit_bytes=1024 * 1024),
    )(*(pltpu.with_memory_space_constraint(result, pltpu.VMEM) for result in results))


def solution(mesh):
    block = P("seq", "head")
    return jax.shard_map(
        functools.partial(local, mesh.shape["seq"], mesh.shape["head"]),
        mesh=mesh,
        in_specs=(block, block, block, block, block, P("head"), P("head"), P()),
        out_specs=(block, block, block),
        check_vma=False,
    )
```

```python
import functools
import math

import jax
import jax.numpy as jnp
from jax import lax
from jax.experimental import pallas as pl
from jax.experimental.pallas import tpu as pltpu
from jax.sharding import PartitionSpec as P

EPSILON = 1e-06
HIDDEN = -1e30
LOG2E = math.log2(math.e)
MESH = pl.DeviceIdType.MESH
NN = (((1,), (0,)), ((), ()))
NT = (((1,), (1,)), ((), ()))


def dot(a, b, dims):
    return lax.dot_general(a, b, dims, preferred_element_type=jnp.float32)


def each(low, high, body):
    if high - low <= 8:
        for j in range(low, high):
            body(j)
    else:

        def step(j, carry):
            body(j)
            return carry

        lax.fori_loop(low, high, step, 0)


def grid_of(n_s):
    root = math.isqrt(n_s)
    return (root, root) if root * root == n_s else (n_s, 1)


def kernel(
    n_s,
    n_h,
    order_hbm,
    q_hbm,
    k_hbm,
    v_hbm,
    o_hbm,
    do_hbm,
    qg_hbm,
    kg_hbm,
    d_q,
    d_k,
    d_v,
    order,
    q_raw,
    k_raw,
    out,
    d_out,
    q_gain,
    k_gain,
    x_t,
    q_scale,
    k_scale,
    qg_t,
    kg_t,
    keys,
    keys_t,
    queries,
    scores,
    dprobs,
    squares,
    q_in,
    k_in,
    q_rows,
    k_rows,
    grads,
    values,
    totals,
    q_moment,
    k_moment,
    dq_out,
    dq_in,
    dk_out,
    dk_in,
    dv_out,
    dv_in,
    inner,
    load,
    sq_send,
    sq_recv,
    qi_send,
    qi_recv,
    ki_send,
    ki_recv,
    qr_send,
    qr_recv,
    kr_send,
    kr_recv,
    gr_send,
    gr_recv,
    va_send,
    va_recv,
    to_send,
    to_recv,
    qm_send,
    qm_recv,
    km_send,
    km_recv,
    dq_send,
    dq_recv,
    dk_send,
    dk_recv,
    dv_send,
    dv_recv,
    inn_send,
    inn_recv,
):
    rows, width = q_raw.shape
    features = n_h * width
    root = width ** (-0.5)
    side, tall = grid_of(n_s)
    me = lax.axis_index("seq")
    mine = lax.axis_index("head")
    my_y, my_x = lax.div(me, side), lax.rem(me, side)

    def row_peer(step):
        return my_y * side + lax.rem(my_x + step, side)

    def column_peer(step):
        return lax.rem(my_y + step, tall) * side + my_x

    def head_peer(step):
        return lax.rem(mine + step, n_h)

    def remote(src, dst, send, recv, j, seq, head):
        return pltpu.make_async_remote_copy(
            src_ref=src,
            dst_ref=dst,
            send_sem=send.at[j],
            recv_sem=recv.at[j],
            device_id=(seq, head),
            device_id_type=MESH,
        )

    def to_row(buffer, send, recv):
        return lambda j: remote(
            buffer.at[0], buffer.at[j], send, recv, j, row_peer(j), mine
        )

    def to_column(buffer, send, recv):
        return lambda j: remote(
            buffer.at[0], buffer.at[j], send, recv, j, column_peer(j), mine
        )

    def to_heads(buffer, send, recv):
        return lambda j: remote(buffer.at[0], buffer.at[j], send, recv, j, me, head_peer(j))

    def back_row(source, target, send, recv):
        return lambda j: remote(
            source.at[j], target.at[j], send, recv, j, row_peer(side - j), mine
        )

    def back_column(source, target, send, recv):
        return lambda j: remote(
            source.at[j], target.at[j], send, recv, j, column_peer(tall - j), mine
        )

    barrier = pltpu.get_barrier_semaphore()

    def greet(seq, head):
        pl.semaphore_signal(barrier, inc=1, device_id=(seq, head), device_id_type=MESH)

    each(1, side, lambda j: greet(row_peer(j), mine))
    each(1, tall, lambda j: greet(column_peer(j), mine))
    each(1, n_h, lambda j: greet(me, head_peer(j)))

    loads = [
        pltpu.make_async_copy(src, dst, load.at[i])
        for i, (src, dst) in enumerate(
            (
                (q_hbm, q_raw),
                (k_hbm, k_raw),
                (do_hbm, d_out),
                (o_hbm, out),
                (qg_hbm, q_gain),
                (kg_hbm, k_gain),
                (v_hbm, values.at[0]),
                (order_hbm, order),
            )
        )
    ]
    for copy in loads:
        copy.start()

    squares_copy = to_heads(squares, sq_send, sq_recv)
    q_copy = to_row(q_in, qi_send, qi_recv)
    k_copy = to_column(k_in, ki_send, ki_recv)
    q_rows_copy = to_row(q_rows, qr_send, qr_recv)
    k_rows_copy = to_column(k_rows, kr_send, kr_recv)
    grads_copy = to_row(grads, gr_send, gr_recv)
    values_copy = to_column(values, va_send, va_recv)
    totals_copy = to_row(totals, to_send, to_recv)
    q_moment_copy = back_row(q_moment.at[0], q_moment.at[1], qm_send, qm_recv)
    k_moment_copy = back_column(k_moment.at[0], k_moment.at[1], km_send, km_recv)
    dq_copy = back_row(dq_out, dq_in, dq_send, dq_recv)
    dk_copy = back_column(dk_out, dk_in, dk_send, dk_recv)
    dv_copy = back_column(dv_out, dv_in, dv_send, dv_recv)
    inner_copy = to_heads(inner, inn_send, inn_recv)

    loads[0].wait()
    x = q_raw[...].astype(jnp.float32).T
    x_t[...] = x
    q_in[0] = x.astype(jnp.bfloat16)
    squares[0, 0:1] = jnp.sum(x * x, axis=0, keepdims=True)
    loads[1].wait()
    y = k_raw[...].astype(jnp.float32).T
    k_in[0] = y.astype(jnp.bfloat16)
    squares[0, 1:2] = jnp.sum(y * y, axis=0, keepdims=True)

    pl.semaphore_wait(barrier, side + tall + n_h - 3)
    each(1, n_h, lambda j: squares_copy(j).start())
    each(1, side, lambda j: q_copy(j).start())
    each(1, tall, lambda j: k_copy(j).start())

    loads[2].wait()
    loads[3].wait()
    grad = d_out[...].astype(jnp.float32)
    grads[0] = grad.T.astype(jnp.bfloat16)
    q_rows[0, 1:2] = jnp.sum((grad * out[...].astype(jnp.float32)).T, axis=0, keepdims=True)
    loads[4].wait()
    loads[5].wait()
    qg_t[...] = jnp.broadcast_to(q_gain[...].astype(jnp.float32), (rows, width)).T
    kg_t[...] = jnp.broadcast_to(k_gain[...].astype(jnp.float32), (rows, width)).T
    loads[6].wait()
    loads[7].wait()

    each(1, n_h, lambda j: squares_copy(j).wait_recv())
    rates = lax.rsqrt(jnp.sum(squares[...], axis=0) / features + EPSILON)
    q_rate, k_rate = rates[0:1], rates[1:2]
    q_rows[0, 0:1] = q_rate
    k_rows[0] = k_rate
    each(1, side, lambda j: q_rows_copy(j).start())
    each(1, tall, lambda j: k_rows_copy(j).start())
    each(1, side, lambda j: grads_copy(j).start())
    each(1, tall, lambda j: values_copy(j).start())

    def form_query(j):
        query = q_in[j].astype(jnp.float32) * q_rows[j, 0:1] * qg_t[...]
        queries[j] = query.astype(jnp.bfloat16)

    def form_keys(j):
        key = k_in[j].astype(jnp.float32) * k_rows[j] * kg_t[...]
        keys_t[j] = key.astype(jnp.bfloat16)
        keys[j] = key.T.astype(jnp.bfloat16)

    row_total = [0.0] * side

    def seen(jx, jy):
        return order[row_peer(side - jx)] >= order[column_peer(tall - jy)]

    def score_tile(jx, jy):
        score = dot(keys[jy], queries[jx], NN) * (root * LOG2E)
        scores[jx, jy] = score
        total = jnp.sum(jnp.exp2(score), axis=0, keepdims=True)
        row_total[jx] += jnp.where(seen(jx, jy), total, 0.0)

    def dprob_tile(jx, jy):
        dprobs[jx, jy] = dot(values[jy], grads[jx], NN) - q_rows[jx, 1:2]

    form_query(0)
    form_keys(0)
    score_tile(0, 0)
    for jx in range(1, side):
        q_copy(jx).wait_recv()
        q_rows_copy(jx).wait_recv()
        form_query(jx)
        score_tile(jx, 0)
    for jy in range(1, tall):
        k_copy(jy).wait_recv()
        k_rows_copy(jy).wait_recv()
        form_keys(jy)
        for jx in range(side):
            score_tile(jx, jy)
    for jx in range(side):
        totals[0, lax.rem(my_x + side - jx, side)] = row_total[jx]
    each(1, side, lambda j: totals_copy(j).start())
    dprob_tile(0, 0)
    q_scale[...] = q_rate * qg_t[...]
    k_scale[...] = (k_rate * kg_t[...]).T
    for jx in range(1, side):
        grads_copy(jx).wait_recv()
        dprob_tile(jx, 0)
    for jy in range(1, tall):
        values_copy(jy).wait_recv()
        for jx in range(side):
            dprob_tile(jx, jy)
    each(1, side, lambda j: totals_copy(j).wait_recv())

    logs = [
        jnp.log2(sum(totals[i, lax.rem(my_x + side - jx, side)] for i in range(side)))
        for jx in range(side)
    ]
    ones = jnp.ones((16, rows), jnp.bfloat16)
    dq = [0.0] * side
    dk = [0.0] * tall
    dv = [0.0] * tall
    q_part = [0.0] * side
    k_part = [0.0] * tall

    def probs_of(jx, jy):
        return jnp.exp2(scores[jx, jy] - jnp.where(seen(jx, jy), logs[jx], -HIDDEN))

    def ds_of(jx, jy, probs):
        ds = probs * dprobs[jx, jy]
        moment = ds * scores[jx, jy]
        q_part[jx] += jnp.sum(moment, axis=0, keepdims=True)
        k_part[jy] += dot(ones, moment.astype(jnp.bfloat16), NT)[0:1]
        return ds.astype(jnp.bfloat16)

    for jy in range(1, tall):
        probs = [probs_of(jx, jy) for jx in range(side)]
        for jx in range(side):
            dv[jy] += dot(probs[jx].astype(jnp.bfloat16), grads[jx], NT)
        dv_out[jy] = dv[jy].astype(jnp.bfloat16)
        dv_copy(jy).start()
        lows = [ds_of(jx, jy, probs[jx]) for jx in range(side)]
        for jx in range(side):
            dk[jy] += dot(lows[jx], queries[jx], NT)
        k_moment[0, jy] = k_part[jy]
        dk_out[jy] = (dk[jy] * root).astype(jnp.bfloat16)
        k_moment_copy(jy).start()
        dk_copy(jy).start()
        for jx in range(side):
            dq[jx] += dot(keys_t[jy], lows[jx], NN)
    for jx in range(1, side):
        probs = probs_of(jx, 0)
        low = ds_of(jx, 0, probs)
        dq[jx] += dot(keys_t[0], low, NN)
        q_moment[0, jx] = q_part[jx]
        dq_out[jx] = (dq[jx] * root).astype(jnp.bfloat16)
        q_moment_copy(jx).start()
        dq_copy(jx).start()
        dk[0] += dot(low, queries[jx], NT)
        dv[0] += dot(probs.astype(jnp.bfloat16), grads[jx], NT)
    probs = probs_of(0, 0)
    low = ds_of(0, 0, probs)

    q_inner, k_inner = q_part[0], k_part[0]
    for jy in range(1, tall):
        k_moment_copy(jy).wait_recv()
        k_inner = k_inner + k_moment[1, jy]
    for jx in range(1, side):
        q_moment_copy(jx).wait_recv()
        q_inner = q_inner + q_moment[1, jx]
    inner[0, 0:1] = q_inner
    inner[0, 1:2] = k_inner
    each(1, n_h, lambda j: inner_copy(j).start())

    own_dv = dv[0] + dot(probs.astype(jnp.bfloat16), grads[0], NT)
    own_dq = (dq[0] + dot(keys_t[0], low, NN)) * root
    own_dk = (dk[0] + dot(low, queries[0], NT)) * root
    for jy in range(1, tall):
        dv_copy(jy).wait_recv()
        own_dv = own_dv + dv_in[jy].astype(jnp.float32)
    d_v[...] = own_dv.astype(jnp.bfloat16)
    for jx in range(1, side):
        dq_copy(jx).wait_recv()
        own_dq = own_dq + dq_in[jx].astype(jnp.float32)
    grad_q = q_scale[...] * own_dq
    each(1, n_h, lambda j: inner_copy(j).wait_recv())
    products = jnp.sum(inner[...], axis=0) * (1.0 / (LOG2E * features))
    grad_q = grad_q - x_t[...] * (q_rate * q_rate * products[0:1])
    d_q[...] = grad_q.T.astype(jnp.bfloat16)
    pull = jnp.broadcast_to(k_rate * k_rate * products[1:2], (width, rows)).T
    for jy in range(1, tall):
        dk_copy(jy).wait_recv()
        own_dk = own_dk + dk_in[jy].astype(jnp.float32)
    d_k[...] = (k_scale[...] * own_dk - k_raw[...].astype(jnp.float32) * pull).astype(jnp.bfloat16)

    for copy in (squares_copy, inner_copy):
        each(1, n_h, lambda j: copy(j).wait_send())
    for copy in (q_copy, q_rows_copy, grads_copy, totals_copy, q_moment_copy, dq_copy):
        each(1, side, lambda j: copy(j).wait_send())
    for copy in (k_copy, k_rows_copy, values_copy, k_moment_copy, dk_copy, dv_copy):
        each(1, tall, lambda j: copy(j).wait_send())


def deliver(*refs):
    sems = refs[6]
    copies = [pltpu.make_async_copy(refs[i], refs[i + 3], sems.at[i]) for i in range(3)]
    for copy in copies:
        copy.start()
    for copy in copies:
        copy.wait()


def local(n_s, n_h, q_raw, k_raw, values, out, d_out, q_gain, k_gain, order):
    rows, width = q_raw.shape
    block = jax.ShapeDtypeStruct((rows, width), jnp.bfloat16)
    vmem = pl.BlockSpec(memory_space=pltpu.VMEM)
    hbm = pl.BlockSpec(memory_space=pltpu.HBM)
    low, wide = jnp.bfloat16, jnp.float32
    side, tall = grid_of(n_s)
    results = pl.pallas_call(
        functools.partial(kernel, n_s, n_h),
        out_shape=(block, block, block),
        in_specs=[hbm] * 8,
        out_specs=(vmem, vmem, vmem),
        scratch_shapes=[
            pltpu.SMEM((n_s,), jnp.int32),
            pltpu.VMEM((rows, width), low),
            pltpu.VMEM((rows, width), low),
            pltpu.VMEM((rows, width), low),
            pltpu.VMEM((rows, width), low),
            pltpu.VMEM((1, width), low),
            pltpu.VMEM((1, width), low),
            pltpu.VMEM((width, rows), wide),
            pltpu.VMEM((width, rows), wide),
            pltpu.VMEM((rows, width), wide),
            pltpu.VMEM((width, rows), wide),
            pltpu.VMEM((width, rows), wide),
            pltpu.VMEM((tall, rows, width), low),
            pltpu.VMEM((tall, width, rows), low),
            pltpu.VMEM((side, width, rows), low),
            pltpu.VMEM((side, tall, rows, rows), wide),
            pltpu.VMEM((side, tall, rows, rows), wide),
            pltpu.VMEM((n_h, 2, rows), wide),
            pltpu.VMEM((side, width, rows), low),
            pltpu.VMEM((tall, width, rows), low),
            pltpu.VMEM((side, 2, rows), wide),
            pltpu.VMEM((tall, 1, rows), wide),
            pltpu.VMEM((side, width, rows), low),
            pltpu.VMEM((tall, rows, width), low),
            pltpu.VMEM((side, side, 1, rows), wide),
            pltpu.VMEM((2, side, 1, rows), wide),
            pltpu.VMEM((2, tall, 1, rows), wide),
            pltpu.VMEM((side, width, rows), low),
            pltpu.VMEM((side, width, rows), low),
            pltpu.VMEM((tall, rows, width), low),
            pltpu.VMEM((tall, rows, width), low),
            pltpu.VMEM((tall, rows, width), low),
            pltpu.VMEM((tall, rows, width), low),
            pltpu.VMEM((n_h, 2, rows), wide),
            pltpu.SemaphoreType.DMA((8,)),
            pltpu.SemaphoreType.DMA((n_h,)),
            pltpu.SemaphoreType.DMA((n_h,)),
            pltpu.SemaphoreType.DMA((side,)),
            pltpu.SemaphoreType.DMA((side,)),
            pltpu.SemaphoreType.DMA((tall,)),
            pltpu.SemaphoreType.DMA((tall,)),
            pltpu.SemaphoreType.DMA((side,)),
            pltpu.SemaphoreType.DMA((side,)),
            pltpu.SemaphoreType.DMA((tall,)),
            pltpu.SemaphoreType.DMA((tall,)),
            pltpu.SemaphoreType.DMA((side,)),
            pltpu.SemaphoreType.DMA((side,)),
            pltpu.SemaphoreType.DMA((tall,)),
            pltpu.SemaphoreType.DMA((tall,)),
            pltpu.SemaphoreType.DMA((side,)),
            pltpu.SemaphoreType.DMA((side,)),
            pltpu.SemaphoreType.DMA((side,)),
            pltpu.SemaphoreType.DMA((side,)),
            pltpu.SemaphoreType.DMA((tall,)),
            pltpu.SemaphoreType.DMA((tall,)),
            pltpu.SemaphoreType.DMA((side,)),
            pltpu.SemaphoreType.DMA((side,)),
            pltpu.SemaphoreType.DMA((tall,)),
            pltpu.SemaphoreType.DMA((tall,)),
            pltpu.SemaphoreType.DMA((tall,)),
            pltpu.SemaphoreType.DMA((tall,)),
            pltpu.SemaphoreType.DMA((n_h,)),
            pltpu.SemaphoreType.DMA((n_h,)),
        ],
        compiler_params=pltpu.CompilerParams(
            collective_id=0, has_side_effects=True, vmem_limit_bytes=40 * 1024 * 1024
        ),
        cost_estimate=pl.CostEstimate(
            flops=10 * n_s * rows * rows * width,
            bytes_accessed=16 * rows * width,
            transcendentals=2 * n_s * rows * rows,
        ),
    )(
        *(
            pltpu.with_memory_space_constraint(array, pltpu.HBM)
            for array in (
                order,
                q_raw,
                k_raw,
                values,
                out,
                d_out,
                q_gain.reshape(1, width),
                k_gain.reshape(1, width),
            )
        )
    )
    return pl.pallas_call(
        deliver,
        out_shape=(block, block, block),
        in_specs=[vmem] * 3,
        out_specs=(hbm, hbm, hbm),
        scratch_shapes=[pltpu.SemaphoreType.DMA((3,))],
        compiler_params=pltpu.CompilerParams(vmem_limit_bytes=1024 * 1024),
    )(*(pltpu.with_memory_space_constraint(result, pltpu.VMEM) for result in results))


def solution(mesh):
    block = P("seq", "head")
    return jax.shard_map(
        functools.partial(local, mesh.shape["seq"], mesh.shape["head"]),
        mesh=mesh,
        in_specs=(block, block, block, block, block, P("head"), P("head"), P()),
        out_specs=(block, block, block),
        check_vma=False,
    )
```

```python
import functools
import math

import jax
import jax.numpy as jnp
from jax import lax
from jax.experimental import pallas as pl
from jax.experimental.pallas import tpu as pltpu
from jax.sharding import PartitionSpec as P

EPSILON = 1e-06
HIDDEN = -1e30
LOG2E = math.log2(math.e)
MESH = pl.DeviceIdType.MESH
NN = (((1,), (0,)), ((), ()))
NT = (((1,), (1,)), ((), ()))


def dot(a, b, dims):
    return lax.dot_general(a, b, dims, preferred_element_type=jnp.float32)


def each(low, high, body):
    if high - low <= 8:
        for j in range(low, high):
            body(j)
    else:

        def step(j, carry):
            body(j)
            return carry

        lax.fori_loop(low, high, step, 0)


def grid_of(n_s):
    root = math.isqrt(n_s)
    return (root, root) if root * root == n_s else (n_s, 1)


def kernel(
    n_s,
    n_h,
    order_hbm,
    q_hbm,
    k_hbm,
    v_hbm,
    o_hbm,
    do_hbm,
    qg_hbm,
    kg_hbm,
    d_q,
    d_k,
    d_v,
    order,
    q_raw,
    k_raw,
    out,
    d_out,
    q_gain,
    k_gain,
    x_t,
    q_scale,
    k_scale,
    qg_t,
    kg_t,
    keys,
    keys_t,
    queries,
    scores,
    dprobs,
    squares,
    up_in,
    up_out,
    down_in,
    down_out,
    q_in,
    k_in,
    q_rows,
    k_rows,
    grads,
    values,
    totals,
    q_moment,
    k_moment,
    dq_out,
    dq_in,
    dk_out,
    dk_in,
    dv_out,
    dv_in,
    inner,
    load,
    sq_send,
    sq_recv,
    qi_send,
    qi_recv,
    ki_send,
    ki_recv,
    qr_send,
    qr_recv,
    kr_send,
    kr_recv,
    gr_send,
    gr_recv,
    va_send,
    va_recv,
    to_send,
    to_recv,
    qm_send,
    qm_recv,
    km_send,
    km_recv,
    dq_send,
    dq_recv,
    dk_send,
    dk_recv,
    dv_send,
    dv_recv,
    inn_send,
    inn_recv,
):
    rows, width = q_raw.shape
    features = n_h * width
    root = width ** (-0.5)
    side, tall = grid_of(n_s)
    me = lax.axis_index("seq")
    mine = lax.axis_index("head")
    my_y, my_x = lax.div(me, side), lax.rem(me, side)

    def row_peer(step):
        return my_y * side + lax.rem(my_x + step, side)

    def column_peer(step):
        return lax.rem(my_y + step, tall) * side + my_x

    level, last = lax.div(mine, 2), n_h // 2 - 1
    twin = level * 2 + 1 - lax.rem(mine, 2)

    def head_peer(step):
        return lax.rem(mine + step, n_h)

    def remote(src, dst, send, recv, j, seq, head):
        return pltpu.make_async_remote_copy(
            src_ref=src,
            dst_ref=dst,
            send_sem=send.at[j],
            recv_sem=recv.at[j],
            device_id=(seq, head),
            device_id_type=MESH,
        )

    def to_row(buffer, send, recv):
        return lambda j: remote(
            buffer.at[0], buffer.at[j], send, recv, j, row_peer(j), mine
        )

    def to_column(buffer, send, recv):
        return lambda j: remote(
            buffer.at[0], buffer.at[j], send, recv, j, column_peer(j), mine
        )

    def to_heads(buffer, send, recv):
        return lambda j: remote(buffer.at[0], buffer.at[j], send, recv, j, me, head_peer(j))

    def back_row(source, target, send, recv):
        return lambda j: remote(
            source.at[j], target.at[j], send, recv, j, row_peer(side - j), mine
        )

    def back_column(source, target, send, recv):
        return lambda j: remote(
            source.at[j], target.at[j], send, recv, j, column_peer(tall - j), mine
        )

    barrier = pltpu.get_barrier_semaphore()

    def greet(seq, head):
        pl.semaphore_signal(barrier, inc=1, device_id=(seq, head), device_id_type=MESH)

    each(1, side, lambda j: greet(row_peer(j), mine))
    each(1, tall, lambda j: greet(column_peer(j), mine))
    greet(me, twin)

    @pl.when(level > 0)
    def _():
        greet(me, mine - 2)

    @pl.when(level < last)
    def _():
        greet(me, mine + 2)


    loads = [
        pltpu.make_async_copy(src, dst, load.at[i])
        for i, (src, dst) in enumerate(
            (
                (q_hbm, q_raw),
                (k_hbm, k_raw),
                (do_hbm, d_out),
                (o_hbm, out),
                (qg_hbm, q_gain),
                (kg_hbm, k_gain),
                (v_hbm, values.at[0]),
                (order_hbm, order),
            )
        )
    ]
    for copy in loads:
        copy.start()

    twin_copy = remote(squares.at[0], squares.at[1], sq_send, sq_recv, 0, me, twin)
    up_copy = remote(up_out, up_in, sq_send, sq_recv, 1, me, mine + 2)
    down_copy = remote(down_out, down_in, sq_send, sq_recv, 2, me, mine - 2)
    q_copy = to_row(q_in, qi_send, qi_recv)
    k_copy = to_column(k_in, ki_send, ki_recv)
    q_rows_copy = to_row(q_rows, qr_send, qr_recv)
    k_rows_copy = to_column(k_rows, kr_send, kr_recv)
    grads_copy = to_row(grads, gr_send, gr_recv)
    values_copy = to_column(values, va_send, va_recv)
    totals_copy = to_row(totals, to_send, to_recv)
    q_moment_copy = back_row(q_moment.at[0], q_moment.at[1], qm_send, qm_recv)
    k_moment_copy = back_column(k_moment.at[0], k_moment.at[1], km_send, km_recv)
    dq_copy = back_row(dq_out, dq_in, dq_send, dq_recv)
    dk_copy = back_column(dk_out, dk_in, dk_send, dk_recv)
    dv_copy = back_column(dv_out, dv_in, dv_send, dv_recv)
    inner_copy = to_heads(inner, inn_send, inn_recv)

    loads[0].wait()
    x = q_raw[...].astype(jnp.float32).T
    x_t[...] = x
    q_in[0] = x.astype(jnp.bfloat16)
    squares[0, 0:1] = jnp.sum(x * x, axis=0, keepdims=True)
    loads[1].wait()
    y = k_raw[...].astype(jnp.float32).T
    k_in[0] = y.astype(jnp.bfloat16)
    squares[0, 1:2] = jnp.sum(y * y, axis=0, keepdims=True)

    below = lax.div(level + last, last + 1)
    above = lax.div(2 * last - level, last + 1)
    pl.semaphore_wait(barrier, side + tall - 1 + below + above)

    twin_copy.start()
    each(1, side, lambda j: q_copy(j).start())
    each(1, tall, lambda j: k_copy(j).start())
    loads[6].wait()
    each(1, tall, lambda j: values_copy(j).start())
    loads[2].wait()
    grad = d_out[...].astype(jnp.float32)
    grads[0] = grad.T.astype(jnp.bfloat16)
    each(1, side, lambda j: grads_copy(j).start())

    loads[3].wait()
    q_rows[0, 1:2] = jnp.sum((grad * out[...].astype(jnp.float32)).T, axis=0, keepdims=True)
    loads[4].wait()
    loads[5].wait()
    qg_t[...] = jnp.broadcast_to(q_gain[...].astype(jnp.float32), (rows, width)).T
    kg_t[...] = jnp.broadcast_to(k_gain[...].astype(jnp.float32), (rows, width)).T
    loads[7].wait()

    twin_copy.wait_recv()
    pair = squares[0] + squares[1]

    @pl.when(level == 0)
    def _():
        up_in[...] = jnp.zeros_like(up_in)

    @pl.when(level > 0)
    def _():
        up_copy.wait_recv()

    @pl.when(level < last)
    def _():
        up_out[...] = up_in[...] + pair
        up_copy.start()

    @pl.when(level == last)
    def _():
        down_in[...] = jnp.zeros_like(down_in)

    @pl.when(level < last)
    def _():
        down_copy.wait_recv()

    @pl.when(level > 0)
    def _():
        down_out[...] = down_in[...] + pair
        down_copy.start()

    rates = lax.rsqrt((pair + up_in[...] + down_in[...]) / features + EPSILON)
    q_rate, k_rate = rates[0:1], rates[1:2]
    q_rows[0, 0:1] = q_rate
    k_rows[0] = k_rate
    each(1, side, lambda j: q_rows_copy(j).start())
    each(1, tall, lambda j: k_rows_copy(j).start())

    def form_query(j):
        query = q_in[j].astype(jnp.float32) * q_rows[j, 0:1] * qg_t[...]
        queries[j] = query.astype(jnp.bfloat16)

    def form_keys(j):
        key = k_in[j].astype(jnp.float32) * k_rows[j] * kg_t[...]
        keys_t[j] = key.astype(jnp.bfloat16)
        keys[j] = key.T.astype(jnp.bfloat16)

    row_total = [0.0] * side

    def seen(jx, jy):
        return order[row_peer(side - jx)] >= order[column_peer(tall - jy)]

    def score_tile(jx, jy):
        score = dot(keys[jy], queries[jx], NN) * (root * LOG2E)
        scores[jx, jy] = score
        total = jnp.sum(jnp.exp2(score), axis=0, keepdims=True)
        row_total[jx] += jnp.where(seen(jx, jy), total, 0.0)

    def dprob_tile(jx, jy):
        dprobs[jx, jy] = dot(values[jy], grads[jx], NN) - q_rows[jx, 1:2]

    form_query(0)
    form_keys(0)
    score_tile(0, 0)
    for jx in range(1, side):
        q_copy(jx).wait_recv()
        q_rows_copy(jx).wait_recv()
        form_query(jx)
        score_tile(jx, 0)
    for jy in range(1, tall):
        k_copy(jy).wait_recv()
        k_rows_copy(jy).wait_recv()
        form_keys(jy)
        for jx in range(side):
            score_tile(jx, jy)
    for jx in range(side):
        totals[0, lax.rem(my_x + side - jx, side)] = row_total[jx]
    each(1, side, lambda j: totals_copy(j).start())
    dprob_tile(0, 0)
    q_scale[...] = q_rate * qg_t[...]
    k_scale[...] = (k_rate * kg_t[...]).T
    for jx in range(1, side):
        grads_copy(jx).wait_recv()
        dprob_tile(jx, 0)
    for jy in range(1, tall):
        values_copy(jy).wait_recv()
        for jx in range(side):
            dprob_tile(jx, jy)
    each(1, side, lambda j: totals_copy(j).wait_recv())

    logs = [
        jnp.log2(sum(totals[i, lax.rem(my_x + side - jx, side)] for i in range(side)))
        for jx in range(side)
    ]
    ones = jnp.ones((16, rows), jnp.bfloat16)
    dq = [0.0] * side
    dk = [0.0] * tall
    dv = [0.0] * tall
    q_part = [0.0] * side
    k_part = [0.0] * tall

    def probs_of(jx, jy):
        return jnp.exp2(scores[jx, jy] - jnp.where(seen(jx, jy), logs[jx], -HIDDEN))

    def ds_of(jx, jy, probs):
        ds = probs * dprobs[jx, jy]
        moment = ds * scores[jx, jy]
        q_part[jx] += jnp.sum(moment, axis=0, keepdims=True)
        k_part[jy] += dot(ones, moment.astype(jnp.bfloat16), NT)[0:1]
        return ds.astype(jnp.bfloat16)

    for jy in range(1, tall):
        probs = [probs_of(jx, jy) for jx in range(side)]
        for jx in range(side):
            dv[jy] += dot(probs[jx].astype(jnp.bfloat16), grads[jx], NT)
        dv_out[jy] = dv[jy].astype(jnp.bfloat16)
        dv_copy(jy).start()
        lows = [ds_of(jx, jy, probs[jx]) for jx in range(side)]
        for jx in range(side):
            dk[jy] += dot(lows[jx], queries[jx], NT)
        k_moment[0, jy] = k_part[jy]
        dk_out[jy] = (dk[jy] * root).astype(jnp.bfloat16)
        k_moment_copy(jy).start()
        dk_copy(jy).start()
        for jx in range(side):
            dq[jx] += dot(keys_t[jy], lows[jx], NN)
    for jx in range(1, side):
        probs = probs_of(jx, 0)
        low = ds_of(jx, 0, probs)
        dq[jx] += dot(keys_t[0], low, NN)
        q_moment[0, jx] = q_part[jx]
        dq_out[jx] = (dq[jx] * root).astype(jnp.bfloat16)
        q_moment_copy(jx).start()
        dq_copy(jx).start()
        dk[0] += dot(low, queries[jx], NT)
        dv[0] += dot(probs.astype(jnp.bfloat16), grads[jx], NT)
    probs = probs_of(0, 0)
    low = ds_of(0, 0, probs)

    q_inner, k_inner = q_part[0], k_part[0]
    for jy in range(1, tall):
        k_moment_copy(jy).wait_recv()
        k_inner = k_inner + k_moment[1, jy]
    for jx in range(1, side):
        q_moment_copy(jx).wait_recv()
        q_inner = q_inner + q_moment[1, jx]
    inner[0, 0:1] = q_inner
    inner[0, 1:2] = k_inner
    each(1, n_h, lambda j: inner_copy(j).start())

    own_dv = dv[0] + dot(probs.astype(jnp.bfloat16), grads[0], NT)
    own_dq = (dq[0] + dot(keys_t[0], low, NN)) * root
    own_dk = (dk[0] + dot(low, queries[0], NT)) * root
    for jy in range(1, tall):
        dv_copy(jy).wait_recv()
        own_dv = own_dv + dv_in[jy].astype(jnp.float32)
    d_v[...] = own_dv.astype(jnp.bfloat16)
    for jx in range(1, side):
        dq_copy(jx).wait_recv()
        own_dq = own_dq + dq_in[jx].astype(jnp.float32)
    grad_q = q_scale[...] * own_dq
    each(1, n_h, lambda j: inner_copy(j).wait_recv())
    products = jnp.sum(inner[...], axis=0) * (1.0 / (LOG2E * features))
    grad_q = grad_q - x_t[...] * (q_rate * q_rate * products[0:1])
    d_q[...] = grad_q.T.astype(jnp.bfloat16)
    pull = jnp.broadcast_to(k_rate * k_rate * products[1:2], (width, rows)).T
    for jy in range(1, tall):
        dk_copy(jy).wait_recv()
        own_dk = own_dk + dk_in[jy].astype(jnp.float32)
    d_k[...] = (k_scale[...] * own_dk - k_raw[...].astype(jnp.float32) * pull).astype(jnp.bfloat16)

    twin_copy.wait_send()

    @pl.when(level < last)
    def _():
        up_copy.wait_send()

    @pl.when(level > 0)
    def _():
        down_copy.wait_send()

    each(1, n_h, lambda j: inner_copy(j).wait_send())
    for copy in (q_copy, q_rows_copy, grads_copy, totals_copy, q_moment_copy, dq_copy):
        each(1, side, lambda j: copy(j).wait_send())
    for copy in (k_copy, k_rows_copy, values_copy, k_moment_copy, dk_copy, dv_copy):
        each(1, tall, lambda j: copy(j).wait_send())


def deliver(*refs):
    sems = refs[6]
    copies = [pltpu.make_async_copy(refs[i], refs[i + 3], sems.at[i]) for i in range(3)]
    for copy in copies:
        copy.start()
    for copy in copies:
        copy.wait()


def local(n_s, n_h, q_raw, k_raw, values, out, d_out, q_gain, k_gain, order):
    rows, width = q_raw.shape
    block = jax.ShapeDtypeStruct((rows, width), jnp.bfloat16)
    vmem = pl.BlockSpec(memory_space=pltpu.VMEM)
    hbm = pl.BlockSpec(memory_space=pltpu.HBM)
    low, wide = jnp.bfloat16, jnp.float32
    side, tall = grid_of(n_s)
    results = pl.pallas_call(
        functools.partial(kernel, n_s, n_h),
        out_shape=(block, block, block),
        in_specs=[hbm] * 8,
        out_specs=(vmem, vmem, vmem),
        scratch_shapes=[
            pltpu.SMEM((n_s,), jnp.int32),
            pltpu.VMEM((rows, width), low),
            pltpu.VMEM((rows, width), low),
            pltpu.VMEM((rows, width), low),
            pltpu.VMEM((rows, width), low),
            pltpu.VMEM((1, width), low),
            pltpu.VMEM((1, width), low),
            pltpu.VMEM((width, rows), wide),
            pltpu.VMEM((width, rows), wide),
            pltpu.VMEM((rows, width), wide),
            pltpu.VMEM((width, rows), wide),
            pltpu.VMEM((width, rows), wide),
            pltpu.VMEM((tall, rows, width), low),
            pltpu.VMEM((tall, width, rows), low),
            pltpu.VMEM((side, width, rows), low),
            pltpu.VMEM((side, tall, rows, rows), wide),
            pltpu.VMEM((side, tall, rows, rows), wide),
            pltpu.VMEM((2, 2, rows), wide),
            pltpu.VMEM((2, rows), wide),
            pltpu.VMEM((2, rows), wide),
            pltpu.VMEM((2, rows), wide),
            pltpu.VMEM((2, rows), wide),
            pltpu.VMEM((side, width, rows), low),
            pltpu.VMEM((tall, width, rows), low),
            pltpu.VMEM((side, 2, rows), wide),
            pltpu.VMEM((tall, 1, rows), wide),
            pltpu.VMEM((side, width, rows), low),
            pltpu.VMEM((tall, rows, width), low),
            pltpu.VMEM((side, side, 1, rows), wide),
            pltpu.VMEM((2, side, 1, rows), wide),
            pltpu.VMEM((2, tall, 1, rows), wide),
            pltpu.VMEM((side, width, rows), low),
            pltpu.VMEM((side, width, rows), low),
            pltpu.VMEM((tall, rows, width), low),
            pltpu.VMEM((tall, rows, width), low),
            pltpu.VMEM((tall, rows, width), low),
            pltpu.VMEM((tall, rows, width), low),
            pltpu.VMEM((n_h, 2, rows), wide),
            pltpu.SemaphoreType.DMA((8,)),
            pltpu.SemaphoreType.DMA((3,)),
            pltpu.SemaphoreType.DMA((3,)),
            pltpu.SemaphoreType.DMA((side,)),
            pltpu.SemaphoreType.DMA((side,)),
            pltpu.SemaphoreType.DMA((tall,)),
            pltpu.SemaphoreType.DMA((tall,)),
            pltpu.SemaphoreType.DMA((side,)),
            pltpu.SemaphoreType.DMA((side,)),
            pltpu.SemaphoreType.DMA((tall,)),
            pltpu.SemaphoreType.DMA((tall,)),
            pltpu.SemaphoreType.DMA((side,)),
            pltpu.SemaphoreType.DMA((side,)),
            pltpu.SemaphoreType.DMA((tall,)),
            pltpu.SemaphoreType.DMA((tall,)),
            pltpu.SemaphoreType.DMA((side,)),
            pltpu.SemaphoreType.DMA((side,)),
            pltpu.SemaphoreType.DMA((side,)),
            pltpu.SemaphoreType.DMA((side,)),
            pltpu.SemaphoreType.DMA((tall,)),
            pltpu.SemaphoreType.DMA((tall,)),
            pltpu.SemaphoreType.DMA((side,)),
            pltpu.SemaphoreType.DMA((side,)),
            pltpu.SemaphoreType.DMA((tall,)),
            pltpu.SemaphoreType.DMA((tall,)),
            pltpu.SemaphoreType.DMA((tall,)),
            pltpu.SemaphoreType.DMA((tall,)),
            pltpu.SemaphoreType.DMA((n_h,)),
            pltpu.SemaphoreType.DMA((n_h,)),
        ],
        compiler_params=pltpu.CompilerParams(
            collective_id=0, has_side_effects=True, vmem_limit_bytes=40 * 1024 * 1024
        ),
        cost_estimate=pl.CostEstimate(
            flops=10 * n_s * rows * rows * width,
            bytes_accessed=16 * rows * width,
            transcendentals=2 * n_s * rows * rows,
        ),
    )(
        *(
            pltpu.with_memory_space_constraint(array, pltpu.HBM)
            for array in (
                order,
                q_raw,
                k_raw,
                values,
                out,
                d_out,
                q_gain.reshape(1, width),
                k_gain.reshape(1, width),
            )
        )
    )
    return pl.pallas_call(
        deliver,
        out_shape=(block, block, block),
        in_specs=[vmem] * 3,
        out_specs=(hbm, hbm, hbm),
        scratch_shapes=[pltpu.SemaphoreType.DMA((3,))],
        compiler_params=pltpu.CompilerParams(vmem_limit_bytes=1024 * 1024),
    )(*(pltpu.with_memory_space_constraint(result, pltpu.VMEM) for result in results))


def solution(mesh):
    block = P("seq", "head")
    return jax.shard_map(
        functools.partial(local, mesh.shape["seq"], mesh.shape["head"]),
        mesh=mesh,
        in_specs=(block, block, block, block, block, P("head"), P("head"), P()),
        out_specs=(block, block, block),
        check_vma=False,
    )
```

```python
import functools
import math

import jax
import jax.numpy as jnp
from jax import lax
from jax.experimental import pallas as pl
from jax.experimental.pallas import tpu as pltpu
from jax.sharding import PartitionSpec as P

EPSILON = 1e-06
HIDDEN = -1e30
LOG2E = math.log2(math.e)
MESH = pl.DeviceIdType.MESH
NN = (((1,), (0,)), ((), ()))
NT = (((1,), (1,)), ((), ()))


def dot(a, b, dims):
    return lax.dot_general(a, b, dims, preferred_element_type=jnp.float32)


def each(low, high, body):
    if high - low <= 8:
        for j in range(low, high):
            body(j)
    else:

        def step(j, carry):
            body(j)
            return carry

        lax.fori_loop(low, high, step, 0)


def grid_of(n_s):
    root = math.isqrt(n_s)
    return (root, root) if root * root == n_s else (n_s, 1)


def kernel(
    n_s,
    n_h,
    order_hbm,
    q_hbm,
    k_hbm,
    v_hbm,
    o_hbm,
    do_hbm,
    qg_hbm,
    kg_hbm,
    d_q,
    d_k,
    d_v,
    order,
    q_raw,
    k_raw,
    out,
    d_out,
    q_gain,
    k_gain,
    x_t,
    q_scale,
    k_scale,
    qg_t,
    kg_t,
    keys,
    keys_t,
    queries,
    scores,
    dprobs,
    squares,
    q_in,
    k_in,
    q_rows,
    k_rows,
    grads,
    values,
    totals,
    q_moment,
    k_moment,
    dq_out,
    dq_in,
    dk_out,
    dk_in,
    dv_out,
    dv_in,
    inner,
    load,
    sq_send,
    sq_recv,
    qi_send,
    qi_recv,
    ki_send,
    ki_recv,
    qr_send,
    qr_recv,
    kr_send,
    kr_recv,
    gr_send,
    gr_recv,
    va_send,
    va_recv,
    to_send,
    to_recv,
    qm_send,
    qm_recv,
    km_send,
    km_recv,
    dq_send,
    dq_recv,
    dk_send,
    dk_recv,
    dv_send,
    dv_recv,
    inn_send,
    inn_recv,
):
    rows, width = q_raw.shape
    features = n_h * width
    root = width ** (-0.5)
    side, tall = grid_of(n_s)
    me = lax.axis_index("seq")
    mine = lax.axis_index("head")
    my_y, my_x = lax.div(me, side), lax.rem(me, side)

    def row_peer(step):
        return my_y * side + lax.rem(my_x + step, side)

    def column_peer(step):
        return lax.rem(my_y + step, tall) * side + my_x

    def head_peer(step):
        return lax.rem(mine + step, n_h)

    def remote(src, dst, send, recv, j, seq, head):
        return pltpu.make_async_remote_copy(
            src_ref=src,
            dst_ref=dst,
            send_sem=send.at[j],
            recv_sem=recv.at[j],
            device_id=(seq, head),
            device_id_type=MESH,
        )

    def to_row(buffer, send, recv):
        return lambda j: remote(
            buffer.at[0], buffer.at[j], send, recv, j, row_peer(j), mine
        )

    def to_column(buffer, send, recv):
        return lambda j: remote(
            buffer.at[0], buffer.at[j], send, recv, j, column_peer(j), mine
        )

    def to_heads(buffer, send, recv):
        return lambda j: remote(buffer.at[0], buffer.at[j], send, recv, j, me, head_peer(j))

    def back_row(source, target, send, recv):
        return lambda j: remote(
            source.at[j], target.at[j], send, recv, j, row_peer(side - j), mine
        )

    def back_column(source, target, send, recv):
        return lambda j: remote(
            source.at[j], target.at[j], send, recv, j, column_peer(tall - j), mine
        )

    barrier = pltpu.get_barrier_semaphore()

    def greet(seq, head):
        pl.semaphore_signal(barrier, inc=1, device_id=(seq, head), device_id_type=MESH)

    each(1, side, lambda j: greet(row_peer(j), mine))
    each(1, tall, lambda j: greet(column_peer(j), mine))
    each(1, n_h, lambda j: greet(me, head_peer(j)))

    loads = [
        pltpu.make_async_copy(src, dst, load.at[i])
        for i, (src, dst) in enumerate(
            (
                (q_hbm, q_raw),
                (k_hbm, k_raw),
                (do_hbm, d_out),
                (o_hbm, out),
                (qg_hbm, q_gain),
                (kg_hbm, k_gain),
                (v_hbm, values.at[0]),
                (order_hbm, order),
            )
        )
    ]
    for copy in loads:
        copy.start()

    squares_copy = to_heads(squares, sq_send, sq_recv)
    q_copy = to_row(q_in, qi_send, qi_recv)
    k_copy = to_column(k_in, ki_send, ki_recv)
    q_rows_copy = to_row(q_rows, qr_send, qr_recv)
    k_rows_copy = to_column(k_rows, kr_send, kr_recv)
    grads_copy = to_row(grads, gr_send, gr_recv)
    values_copy = to_column(values, va_send, va_recv)
    totals_copy = to_row(totals, to_send, to_recv)
    q_moment_copy = back_row(q_moment.at[0], q_moment.at[1], qm_send, qm_recv)
    k_moment_copy = back_column(k_moment.at[0], k_moment.at[1], km_send, km_recv)
    dq_copy = back_row(dq_out, dq_in, dq_send, dq_recv)
    dk_copy = back_column(dk_out, dk_in, dk_send, dk_recv)
    dv_copy = back_column(dv_out, dv_in, dv_send, dv_recv)
    inner_copy = to_heads(inner, inn_send, inn_recv)

    loads[0].wait()
    x = q_raw[...].astype(jnp.float32).T
    x_t[...] = x
    q_in[0] = x.astype(jnp.bfloat16)
    squares[0, 0:1] = jnp.sum(x * x, axis=0, keepdims=True)
    loads[1].wait()
    y = k_raw[...].astype(jnp.float32).T
    k_in[0] = y.astype(jnp.bfloat16)
    squares[0, 1:2] = jnp.sum(y * y, axis=0, keepdims=True)

    pl.semaphore_wait(barrier, side + tall + n_h - 3)
    each(1, n_h, lambda j: squares_copy(j).start())
    each(1, side, lambda j: q_copy(j).start())
    each(1, tall, lambda j: k_copy(j).start())

    loads[2].wait()
    loads[3].wait()
    grad = d_out[...].astype(jnp.float32)
    grads[0] = grad.T.astype(jnp.bfloat16)
    q_rows[0, 1:2] = jnp.sum((grad * out[...].astype(jnp.float32)).T, axis=0, keepdims=True)
    loads[4].wait()
    loads[5].wait()
    qg_t[...] = jnp.broadcast_to(q_gain[...].astype(jnp.float32), (rows, width)).T
    kg_t[...] = jnp.broadcast_to(k_gain[...].astype(jnp.float32), (rows, width)).T
    loads[6].wait()
    loads[7].wait()

    each(1, n_h, lambda j: squares_copy(j).wait_recv())
    rates = lax.rsqrt(jnp.sum(squares[...], axis=0) / features + EPSILON)
    q_rate, k_rate = rates[0:1], rates[1:2]
    q_rows[0, 0:1] = q_rate
    k_rows[0] = k_rate
    each(1, side, lambda j: q_rows_copy(j).start())
    each(1, tall, lambda j: k_rows_copy(j).start())
    each(1, side, lambda j: grads_copy(j).start())
    each(1, tall, lambda j: values_copy(j).start())

    def form_query(j):
        query = q_in[j].astype(jnp.float32) * q_rows[j, 0:1] * qg_t[...]
        queries[j] = query.astype(jnp.bfloat16)

    def form_keys(j):
        key = k_in[j].astype(jnp.float32) * k_rows[j] * kg_t[...]
        keys_t[j] = key.astype(jnp.bfloat16)
        keys[j] = key.T.astype(jnp.bfloat16)

    row_total = [0.0] * side

    def seen(jx, jy):
        return order[row_peer(side - jx)] >= order[column_peer(tall - jy)]

    def score_tile(jx, jy):
        score = dot(keys[jy], queries[jx], NN) * (root * LOG2E)
        scores[jx, jy] = score
        total = jnp.sum(jnp.exp2(score), axis=0, keepdims=True)
        row_total[jx] += jnp.where(seen(jx, jy), total, 0.0)

    def dprob_tile(jx, jy):
        dprobs[jx, jy] = dot(values[jy], grads[jx], NN) - q_rows[jx, 1:2]

    form_query(0)
    form_keys(0)
    score_tile(0, 0)
    for jx in range(1, side):
        q_copy(jx).wait_recv()
        q_rows_copy(jx).wait_recv()
        form_query(jx)
        score_tile(jx, 0)
    for jy in range(1, tall):
        k_copy(jy).wait_recv()
        k_rows_copy(jy).wait_recv()
        form_keys(jy)
        for jx in range(side):
            score_tile(jx, jy)
    for jx in range(side):
        totals[0, lax.rem(my_x + side - jx, side)] = row_total[jx]
    each(1, side, lambda j: totals_copy(j).start())
    dprob_tile(0, 0)
    q_scale[...] = q_rate * qg_t[...]
    k_scale[...] = (k_rate * kg_t[...]).T
    for jx in range(1, side):
        grads_copy(jx).wait_recv()
        dprob_tile(jx, 0)
    for jy in range(1, tall):
        values_copy(jy).wait_recv()
        for jx in range(side):
            dprob_tile(jx, jy)
    each(1, side, lambda j: totals_copy(j).wait_recv())

    logs = [
        jnp.log2(sum(totals[i, lax.rem(my_x + side - jx, side)] for i in range(side)))
        for jx in range(side)
    ]
    ones = jnp.ones((16, rows), jnp.bfloat16)
    dq = [0.0] * side
    dk = [0.0] * tall
    dv = [0.0] * tall
    q_part = [0.0] * side
    k_part = [0.0] * tall

    def probs_of(jx, jy):
        return jnp.exp2(scores[jx, jy] - jnp.where(seen(jx, jy), logs[jx], -HIDDEN))

    def ds_of(jx, jy, probs):
        ds = probs * dprobs[jx, jy]
        moment = ds * scores[jx, jy]
        q_part[jx] += jnp.sum(moment, axis=0, keepdims=True)
        k_part[jy] += dot(ones, moment.astype(jnp.bfloat16), NT)[0:1]
        return ds.astype(jnp.bfloat16)

    probs, lows = {}, {}
    tiles = [(jx, jy) for jy in range(tall) for jx in range(side)][1:]
    for jx, jy in tiles:
        probs[jx, jy] = probs_of(jx, jy)
        lows[jx, jy] = ds_of(jx, jy, probs[jx, jy])
        probs[jx, jy] = probs[jx, jy].astype(jnp.bfloat16)
    for jy in range(1, tall):
        k_moment[0, jy] = k_part[jy]
        k_moment_copy(jy).start()
    for jx in range(1, side):
        q_moment[0, jx] = q_part[jx]
        q_moment_copy(jx).start()
    for jy in range(1, tall):
        for jx in range(side):
            dv[jy] += dot(probs[jx, jy], grads[jx], NT)
        dv_out[jy] = dv[jy].astype(jnp.bfloat16)
        dv_copy(jy).start()
    for jx in range(1, side):
        for jy in range(tall):
            dq[jx] += dot(keys_t[jy], lows[jx, jy], NN)
        dq_out[jx] = (dq[jx] * root).astype(jnp.bfloat16)
        dq_copy(jx).start()
    probs[0, 0] = probs_of(0, 0)
    lows[0, 0] = ds_of(0, 0, probs[0, 0])
    probs[0, 0] = probs[0, 0].astype(jnp.bfloat16)
    for jy in range(1, tall):
        for jx in range(side):
            dk[jy] += dot(lows[jx, jy], queries[jx], NT)
        dk_out[jy] = (dk[jy] * root).astype(jnp.bfloat16)

    q_inner, k_inner = q_part[0], k_part[0]
    for jy in range(1, tall):
        k_moment_copy(jy).wait_recv()
        k_inner = k_inner + k_moment[1, jy]
    for jx in range(1, side):
        q_moment_copy(jx).wait_recv()
        q_inner = q_inner + q_moment[1, jx]
    inner[0, 0:1] = q_inner
    inner[0, 1:2] = k_inner
    each(1, n_h, lambda j: inner_copy(j).start())
    each(1, tall, lambda j: dk_copy(j).start())

    for jy in range(tall):
        dq[0] += dot(keys_t[jy], lows[0, jy], NN)
    for jx in range(side):
        dk[0] += dot(lows[jx, 0], queries[jx], NT)
        dv[0] += dot(probs[jx, 0], grads[jx], NT)
    own_dv, own_dq, own_dk = dv[0], dq[0] * root, dk[0] * root
    for jy in range(1, tall):
        dv_copy(jy).wait_recv()
        own_dv = own_dv + dv_in[jy].astype(jnp.float32)
    d_v[...] = own_dv.astype(jnp.bfloat16)
    for jx in range(1, side):
        dq_copy(jx).wait_recv()
        own_dq = own_dq + dq_in[jx].astype(jnp.float32)
    grad_q = q_scale[...] * own_dq
    each(1, n_h, lambda j: inner_copy(j).wait_recv())
    products = jnp.sum(inner[...], axis=0) * (1.0 / (LOG2E * features))
    grad_q = grad_q - x_t[...] * (q_rate * q_rate * products[0:1])
    d_q[...] = grad_q.T.astype(jnp.bfloat16)
    pull = jnp.broadcast_to(k_rate * k_rate * products[1:2], (width, rows)).T
    for jy in range(1, tall):
        dk_copy(jy).wait_recv()
        own_dk = own_dk + dk_in[jy].astype(jnp.float32)
    d_k[...] = (k_scale[...] * own_dk - k_raw[...].astype(jnp.float32) * pull).astype(jnp.bfloat16)

    for copy in (squares_copy, inner_copy):
        each(1, n_h, lambda j: copy(j).wait_send())
    for copy in (q_copy, q_rows_copy, grads_copy, totals_copy, q_moment_copy, dq_copy):
        each(1, side, lambda j: copy(j).wait_send())
    for copy in (k_copy, k_rows_copy, values_copy, k_moment_copy, dk_copy, dv_copy):
        each(1, tall, lambda j: copy(j).wait_send())


def deliver(*refs):
    sems = refs[6]
    copies = [pltpu.make_async_copy(refs[i], refs[i + 3], sems.at[i]) for i in range(3)]
    for copy in copies:
        copy.start()
    for copy in copies:
        copy.wait()


def local(n_s, n_h, q_raw, k_raw, values, out, d_out, q_gain, k_gain, order):
    rows, width = q_raw.shape
    block = jax.ShapeDtypeStruct((rows, width), jnp.bfloat16)
    vmem = pl.BlockSpec(memory_space=pltpu.VMEM)
    hbm = pl.BlockSpec(memory_space=pltpu.HBM)
    low, wide = jnp.bfloat16, jnp.float32
    side, tall = grid_of(n_s)
    results = pl.pallas_call(
        functools.partial(kernel, n_s, n_h),
        out_shape=(block, block, block),
        in_specs=[hbm] * 8,
        out_specs=(vmem, vmem, vmem),
        scratch_shapes=[
            pltpu.SMEM((n_s,), jnp.int32),
            pltpu.VMEM((rows, width), low),
            pltpu.VMEM((rows, width), low),
            pltpu.VMEM((rows, width), low),
            pltpu.VMEM((rows, width), low),
            pltpu.VMEM((1, width), low),
            pltpu.VMEM((1, width), low),
            pltpu.VMEM((width, rows), wide),
            pltpu.VMEM((width, rows), wide),
            pltpu.VMEM((rows, width), wide),
            pltpu.VMEM((width, rows), wide),
            pltpu.VMEM((width, rows), wide),
            pltpu.VMEM((tall, rows, width), low),
            pltpu.VMEM((tall, width, rows), low),
            pltpu.VMEM((side, width, rows), low),
            pltpu.VMEM((side, tall, rows, rows), wide),
            pltpu.VMEM((side, tall, rows, rows), wide),
            pltpu.VMEM((n_h, 2, rows), wide),
            pltpu.VMEM((side, width, rows), low),
            pltpu.VMEM((tall, width, rows), low),
            pltpu.VMEM((side, 2, rows), wide),
            pltpu.VMEM((tall, 1, rows), wide),
            pltpu.VMEM((side, width, rows), low),
            pltpu.VMEM((tall, rows, width), low),
            pltpu.VMEM((side, side, 1, rows), wide),
            pltpu.VMEM((2, side, 1, rows), wide),
            pltpu.VMEM((2, tall, 1, rows), wide),
            pltpu.VMEM((side, width, rows), low),
            pltpu.VMEM((side, width, rows), low),
            pltpu.VMEM((tall, rows, width), low),
            pltpu.VMEM((tall, rows, width), low),
            pltpu.VMEM((tall, rows, width), low),
            pltpu.VMEM((tall, rows, width), low),
            pltpu.VMEM((n_h, 2, rows), wide),
            pltpu.SemaphoreType.DMA((8,)),
            pltpu.SemaphoreType.DMA((n_h,)),
            pltpu.SemaphoreType.DMA((n_h,)),
            pltpu.SemaphoreType.DMA((side,)),
            pltpu.SemaphoreType.DMA((side,)),
            pltpu.SemaphoreType.DMA((tall,)),
            pltpu.SemaphoreType.DMA((tall,)),
            pltpu.SemaphoreType.DMA((side,)),
            pltpu.SemaphoreType.DMA((side,)),
            pltpu.SemaphoreType.DMA((tall,)),
            pltpu.SemaphoreType.DMA((tall,)),
            pltpu.SemaphoreType.DMA((side,)),
            pltpu.SemaphoreType.DMA((side,)),
            pltpu.SemaphoreType.DMA((tall,)),
            pltpu.SemaphoreType.DMA((tall,)),
            pltpu.SemaphoreType.DMA((side,)),
            pltpu.SemaphoreType.DMA((side,)),
            pltpu.SemaphoreType.DMA((side,)),
            pltpu.SemaphoreType.DMA((side,)),
            pltpu.SemaphoreType.DMA((tall,)),
            pltpu.SemaphoreType.DMA((tall,)),
            pltpu.SemaphoreType.DMA((side,)),
            pltpu.SemaphoreType.DMA((side,)),
            pltpu.SemaphoreType.DMA((tall,)),
            pltpu.SemaphoreType.DMA((tall,)),
            pltpu.SemaphoreType.DMA((tall,)),
            pltpu.SemaphoreType.DMA((tall,)),
            pltpu.SemaphoreType.DMA((n_h,)),
            pltpu.SemaphoreType.DMA((n_h,)),
        ],
        compiler_params=pltpu.CompilerParams(
            collective_id=0, has_side_effects=True, vmem_limit_bytes=40 * 1024 * 1024
        ),
        cost_estimate=pl.CostEstimate(
            flops=10 * n_s * rows * rows * width,
            bytes_accessed=16 * rows * width,
            transcendentals=2 * n_s * rows * rows,
        ),
    )(
        *(
            pltpu.with_memory_space_constraint(array, pltpu.HBM)
            for array in (
                order,
                q_raw,
                k_raw,
                values,
                out,
                d_out,
                q_gain.reshape(1, width),
                k_gain.reshape(1, width),
            )
        )
    )
    return pl.pallas_call(
        deliver,
        out_shape=(block, block, block),
        in_specs=[vmem] * 3,
        out_specs=(hbm, hbm, hbm),
        scratch_shapes=[pltpu.SemaphoreType.DMA((3,))],
        compiler_params=pltpu.CompilerParams(vmem_limit_bytes=1024 * 1024),
    )(*(pltpu.with_memory_space_constraint(result, pltpu.VMEM) for result in results))


def solution(mesh):
    block = P("seq", "head")
    return jax.shard_map(
        functools.partial(local, mesh.shape["seq"], mesh.shape["head"]),
        mesh=mesh,
        in_specs=(block, block, block, block, block, P("head"), P("head"), P()),
        out_specs=(block, block, block),
        check_vma=False,
    )
```

```python
import functools
import math

import jax
import jax.numpy as jnp
from jax import lax
from jax.experimental import pallas as pl
from jax.experimental.pallas import tpu as pltpu
from jax.sharding import PartitionSpec as P

EPSILON = 1e-06
HIDDEN = -1e30
LOG2E = math.log2(math.e)
MESH = pl.DeviceIdType.MESH
NN = (((1,), (0,)), ((), ()))
NT = (((1,), (1,)), ((), ()))


def dot(a, b, dims):
    return lax.dot_general(a, b, dims, preferred_element_type=jnp.float32)


def each(low, high, body):
    if high - low <= 8:
        for j in range(low, high):
            body(j)
    else:

        def step(j, carry):
            body(j)
            return carry

        lax.fori_loop(low, high, step, 0)


def grid_of(n_s):
    root = math.isqrt(n_s)
    return (root, root) if root * root == n_s else (n_s, 1)


def kernel(
    n_s,
    n_h,
    order_hbm,
    q_hbm,
    k_hbm,
    v_hbm,
    o_hbm,
    do_hbm,
    qg_hbm,
    kg_hbm,
    d_q,
    d_k,
    d_v,
    order,
    q_raw,
    k_raw,
    out,
    d_out,
    q_gain,
    k_gain,
    x_t,
    q_scale,
    k_scale,
    qg_t,
    kg_t,
    keys,
    keys_t,
    queries,
    scores,
    dprobs,
    squares,
    q_in,
    k_in,
    q_rows,
    k_rows,
    grads,
    values,
    totals,
    q_moment,
    k_moment,
    dq_out,
    dq_in,
    dk_out,
    dk_in,
    dv_out,
    dv_in,
    inner,
    load,
    sq_send,
    sq_recv,
    qi_send,
    qi_recv,
    ki_send,
    ki_recv,
    qr_send,
    qr_recv,
    kr_send,
    kr_recv,
    gr_send,
    gr_recv,
    va_send,
    va_recv,
    to_send,
    to_recv,
    qm_send,
    qm_recv,
    km_send,
    km_recv,
    dq_send,
    dq_recv,
    dk_send,
    dk_recv,
    dv_send,
    dv_recv,
    inn_send,
    inn_recv,
):
    rows, width = q_raw.shape
    features = n_h * width
    root = width ** (-0.5)
    side, tall = grid_of(n_s)
    me = lax.axis_index("seq")
    mine = lax.axis_index("head")
    my_y, my_x = lax.div(me, side), lax.rem(me, side)

    def row_peer(step):
        return my_y * side + lax.rem(my_x + step, side)

    def column_peer(step):
        return lax.rem(my_y + step, tall) * side + my_x

    def head_peer(step):
        return lax.rem(mine + step, n_h)

    def remote(src, dst, send, recv, j, seq, head):
        return pltpu.make_async_remote_copy(
            src_ref=src,
            dst_ref=dst,
            send_sem=send.at[j],
            recv_sem=recv.at[j],
            device_id=(seq, head),
            device_id_type=MESH,
        )

    def to_row(buffer, send, recv):
        return lambda j: remote(
            buffer.at[0], buffer.at[j], send, recv, j, row_peer(j), mine
        )

    def to_column(buffer, send, recv):
        return lambda j: remote(
            buffer.at[0], buffer.at[j], send, recv, j, column_peer(j), mine
        )

    def to_heads(buffer, send, recv):
        return lambda j: remote(buffer.at[0], buffer.at[j], send, recv, j, me, head_peer(j))

    def back_row(source, target, send, recv):
        return lambda j: remote(
            source.at[j], target.at[j], send, recv, j, row_peer(side - j), mine
        )

    def back_column(source, target, send, recv):
        return lambda j: remote(
            source.at[j], target.at[j], send, recv, j, column_peer(tall - j), mine
        )

    barrier = pltpu.get_barrier_semaphore()

    def greet(seq, head):
        pl.semaphore_signal(barrier, inc=1, device_id=(seq, head), device_id_type=MESH)

    each(1, side, lambda j: greet(row_peer(j), mine))
    each(1, tall, lambda j: greet(column_peer(j), mine))
    each(1, n_h, lambda j: greet(me, head_peer(j)))

    loads = [
        pltpu.make_async_copy(src, dst, load.at[i])
        for i, (src, dst) in enumerate(
            (
                (q_hbm, q_raw),
                (k_hbm, k_raw),
                (do_hbm, d_out),
                (o_hbm, out),
                (qg_hbm, q_gain),
                (kg_hbm, k_gain),
                (v_hbm, values.at[0]),
                (order_hbm, order),
            )
        )
    ]
    for copy in loads:
        copy.start()

    squares_copy = to_heads(squares, sq_send, sq_recv)
    q_copy = to_row(q_in, qi_send, qi_recv)
    k_copy = to_column(k_in, ki_send, ki_recv)
    q_rows_copy = to_row(q_rows, qr_send, qr_recv)
    k_rows_copy = to_column(k_rows, kr_send, kr_recv)
    grads_copy = to_row(grads, gr_send, gr_recv)
    values_copy = to_column(values, va_send, va_recv)
    totals_copy = to_row(totals, to_send, to_recv)
    q_moment_copy = back_row(q_moment.at[0], q_moment.at[1], qm_send, qm_recv)
    k_moment_copy = back_column(k_moment.at[0], k_moment.at[1], km_send, km_recv)
    dq_copy = back_row(dq_out, dq_in, dq_send, dq_recv)
    dk_copy = back_column(dk_out, dk_in, dk_send, dk_recv)
    dv_copy = back_column(dv_out, dv_in, dv_send, dv_recv)
    inner_copy = to_heads(inner, inn_send, inn_recv)

    def alternate(along_row, along_column):
        @pl.when(lax.rem(mine, 2) == 0)
        def _():
            each(1, side, lambda j: along_row(j).start())
            each(1, tall, lambda j: along_column(j).start())

        @pl.when(lax.rem(mine, 2) == 1)
        def _():
            each(1, tall, lambda j: along_column(j).start())
            each(1, side, lambda j: along_row(j).start())

    loads[0].wait()
    x = q_raw[...].astype(jnp.float32).T
    x_t[...] = x
    q_in[0] = x.astype(jnp.bfloat16)
    squares[0, 0:1] = jnp.sum(x * x, axis=0, keepdims=True)
    loads[1].wait()
    y = k_raw[...].astype(jnp.float32).T
    k_in[0] = y.astype(jnp.bfloat16)
    squares[0, 1:2] = jnp.sum(y * y, axis=0, keepdims=True)

    pl.semaphore_wait(barrier, side + tall + n_h - 3)
    each(1, n_h, lambda j: squares_copy(j).start())
    alternate(q_copy, k_copy)

    loads[2].wait()
    loads[3].wait()
    grad = d_out[...].astype(jnp.float32)
    grads[0] = grad.T.astype(jnp.bfloat16)
    q_rows[0, 1:2] = jnp.sum((grad * out[...].astype(jnp.float32)).T, axis=0, keepdims=True)
    loads[4].wait()
    loads[5].wait()
    qg_t[...] = jnp.broadcast_to(q_gain[...].astype(jnp.float32), (rows, width)).T
    kg_t[...] = jnp.broadcast_to(k_gain[...].astype(jnp.float32), (rows, width)).T
    loads[6].wait()
    loads[7].wait()

    each(1, n_h, lambda j: squares_copy(j).wait_recv())
    rates = lax.rsqrt(jnp.sum(squares[...], axis=0) / features + EPSILON)
    q_rate, k_rate = rates[0:1], rates[1:2]
    q_rows[0, 0:1] = q_rate
    k_rows[0] = k_rate
    each(1, side, lambda j: q_rows_copy(j).start())
    each(1, tall, lambda j: k_rows_copy(j).start())
    alternate(grads_copy, values_copy)

    def form_query(j):
        query = q_in[j].astype(jnp.float32) * q_rows[j, 0:1] * qg_t[...]
        queries[j] = query.astype(jnp.bfloat16)

    def form_keys(j):
        key = k_in[j].astype(jnp.float32) * k_rows[j] * kg_t[...]
        keys_t[j] = key.astype(jnp.bfloat16)
        keys[j] = key.T.astype(jnp.bfloat16)

    row_total = [0.0] * side

    def seen(jx, jy):
        return order[row_peer(side - jx)] >= order[column_peer(tall - jy)]

    def score_tile(jx, jy):
        score = dot(keys[jy], queries[jx], NN) * (root * LOG2E)
        scores[jx, jy] = score
        total = jnp.sum(jnp.exp2(score), axis=0, keepdims=True)
        row_total[jx] += jnp.where(seen(jx, jy), total, 0.0)

    def dprob_tile(jx, jy):
        dprobs[jx, jy] = dot(values[jy], grads[jx], NN) - q_rows[jx, 1:2]

    form_query(0)
    form_keys(0)
    score_tile(0, 0)
    for jx in range(1, side):
        q_copy(jx).wait_recv()
        q_rows_copy(jx).wait_recv()
        form_query(jx)
        score_tile(jx, 0)
    for jy in range(1, tall):
        k_copy(jy).wait_recv()
        k_rows_copy(jy).wait_recv()
        form_keys(jy)
        for jx in range(side):
            score_tile(jx, jy)
    for jx in range(side):
        totals[0, lax.rem(my_x + side - jx, side)] = row_total[jx]
    each(1, side, lambda j: totals_copy(j).start())
    dprob_tile(0, 0)
    q_scale[...] = q_rate * qg_t[...]
    k_scale[...] = (k_rate * kg_t[...]).T
    for jx in range(1, side):
        grads_copy(jx).wait_recv()
        dprob_tile(jx, 0)
    for jy in range(1, tall):
        values_copy(jy).wait_recv()
        for jx in range(side):
            dprob_tile(jx, jy)
    each(1, side, lambda j: totals_copy(j).wait_recv())

    logs = [
        jnp.log2(sum(totals[i, lax.rem(my_x + side - jx, side)] for i in range(side)))
        for jx in range(side)
    ]
    ones = jnp.ones((16, rows), jnp.bfloat16)
    dq = [0.0] * side
    dk = [0.0] * tall
    dv = [0.0] * tall
    q_part = [0.0] * side
    k_part = [0.0] * tall

    def probs_of(jx, jy):
        return jnp.exp2(scores[jx, jy] - jnp.where(seen(jx, jy), logs[jx], -HIDDEN))

    def ds_of(jx, jy, probs):
        ds = probs * dprobs[jx, jy]
        moment = ds * scores[jx, jy]
        q_part[jx] += jnp.sum(moment, axis=0, keepdims=True)
        k_part[jy] += dot(ones, moment.astype(jnp.bfloat16), NT)[0:1]
        return ds.astype(jnp.bfloat16)

    probs, lows = {}, {}
    tiles = [(jx, jy) for jy in range(tall) for jx in range(side)][1:]
    for jx, jy in tiles:
        probs[jx, jy] = probs_of(jx, jy)
        lows[jx, jy] = ds_of(jx, jy, probs[jx, jy])
        probs[jx, jy] = probs[jx, jy].astype(jnp.bfloat16)
    for jy in range(1, tall):
        k_moment[0, jy] = k_part[jy]
        k_moment_copy(jy).start()
    for jx in range(1, side):
        q_moment[0, jx] = q_part[jx]
        q_moment_copy(jx).start()
    for jy in range(1, tall):
        for jx in range(side):
            dv[jy] += dot(probs[jx, jy], grads[jx], NT)
        dv_out[jy] = dv[jy].astype(jnp.bfloat16)
    for jx in range(1, side):
        for jy in range(tall):
            dq[jx] += dot(keys_t[jy], lows[jx, jy], NN)
        dq_out[jx] = (dq[jx] * root).astype(jnp.bfloat16)
    alternate(dq_copy, dv_copy)
    probs[0, 0] = probs_of(0, 0)
    lows[0, 0] = ds_of(0, 0, probs[0, 0])
    probs[0, 0] = probs[0, 0].astype(jnp.bfloat16)
    for jy in range(1, tall):
        for jx in range(side):
            dk[jy] += dot(lows[jx, jy], queries[jx], NT)
        dk_out[jy] = (dk[jy] * root).astype(jnp.bfloat16)

    q_inner, k_inner = q_part[0], k_part[0]
    for jy in range(1, tall):
        k_moment_copy(jy).wait_recv()
        k_inner = k_inner + k_moment[1, jy]
    for jx in range(1, side):
        q_moment_copy(jx).wait_recv()
        q_inner = q_inner + q_moment[1, jx]
    inner[0, 0:1] = q_inner
    inner[0, 1:2] = k_inner
    each(1, n_h, lambda j: inner_copy(j).start())
    each(1, tall, lambda j: dk_copy(j).start())

    for jy in range(tall):
        dq[0] += dot(keys_t[jy], lows[0, jy], NN)
    for jx in range(side):
        dk[0] += dot(lows[jx, 0], queries[jx], NT)
        dv[0] += dot(probs[jx, 0], grads[jx], NT)
    own_dv, own_dq, own_dk = dv[0], dq[0] * root, dk[0] * root
    for jy in range(1, tall):
        dv_copy(jy).wait_recv()
        own_dv = own_dv + dv_in[jy].astype(jnp.float32)
    d_v[...] = own_dv.astype(jnp.bfloat16)
    for jx in range(1, side):
        dq_copy(jx).wait_recv()
        own_dq = own_dq + dq_in[jx].astype(jnp.float32)
    grad_q = q_scale[...] * own_dq
    each(1, n_h, lambda j: inner_copy(j).wait_recv())
    products = jnp.sum(inner[...], axis=0) * (1.0 / (LOG2E * features))
    grad_q = grad_q - x_t[...] * (q_rate * q_rate * products[0:1])
    d_q[...] = grad_q.T.astype(jnp.bfloat16)
    pull = jnp.broadcast_to(k_rate * k_rate * products[1:2], (width, rows)).T
    for jy in range(1, tall):
        dk_copy(jy).wait_recv()
        own_dk = own_dk + dk_in[jy].astype(jnp.float32)
    d_k[...] = (k_scale[...] * own_dk - k_raw[...].astype(jnp.float32) * pull).astype(jnp.bfloat16)

    for copy in (squares_copy, inner_copy):
        each(1, n_h, lambda j: copy(j).wait_send())
    for copy in (q_copy, q_rows_copy, grads_copy, totals_copy, q_moment_copy, dq_copy):
        each(1, side, lambda j: copy(j).wait_send())
    for copy in (k_copy, k_rows_copy, values_copy, k_moment_copy, dk_copy, dv_copy):
        each(1, tall, lambda j: copy(j).wait_send())


def deliver(*refs):
    sems = refs[6]
    copies = [pltpu.make_async_copy(refs[i], refs[i + 3], sems.at[i]) for i in range(3)]
    for copy in copies:
        copy.start()
    for copy in copies:
        copy.wait()


def local(n_s, n_h, q_raw, k_raw, values, out, d_out, q_gain, k_gain, order):
    rows, width = q_raw.shape
    block = jax.ShapeDtypeStruct((rows, width), jnp.bfloat16)
    vmem = pl.BlockSpec(memory_space=pltpu.VMEM)
    hbm = pl.BlockSpec(memory_space=pltpu.HBM)
    low, wide = jnp.bfloat16, jnp.float32
    side, tall = grid_of(n_s)
    results = pl.pallas_call(
        functools.partial(kernel, n_s, n_h),
        out_shape=(block, block, block),
        in_specs=[hbm] * 8,
        out_specs=(vmem, vmem, vmem),
        scratch_shapes=[
            pltpu.SMEM((n_s,), jnp.int32),
            pltpu.VMEM((rows, width), low),
            pltpu.VMEM((rows, width), low),
            pltpu.VMEM((rows, width), low),
            pltpu.VMEM((rows, width), low),
            pltpu.VMEM((1, width), low),
            pltpu.VMEM((1, width), low),
            pltpu.VMEM((width, rows), wide),
            pltpu.VMEM((width, rows), wide),
            pltpu.VMEM((rows, width), wide),
            pltpu.VMEM((width, rows), wide),
            pltpu.VMEM((width, rows), wide),
            pltpu.VMEM((tall, rows, width), low),
            pltpu.VMEM((tall, width, rows), low),
            pltpu.VMEM((side, width, rows), low),
            pltpu.VMEM((side, tall, rows, rows), wide),
            pltpu.VMEM((side, tall, rows, rows), wide),
            pltpu.VMEM((n_h, 2, rows), wide),
            pltpu.VMEM((side, width, rows), low),
            pltpu.VMEM((tall, width, rows), low),
            pltpu.VMEM((side, 2, rows), wide),
            pltpu.VMEM((tall, 1, rows), wide),
            pltpu.VMEM((side, width, rows), low),
            pltpu.VMEM((tall, rows, width), low),
            pltpu.VMEM((side, side, 1, rows), wide),
            pltpu.VMEM((2, side, 1, rows), wide),
            pltpu.VMEM((2, tall, 1, rows), wide),
            pltpu.VMEM((side, width, rows), low),
            pltpu.VMEM((side, width, rows), low),
            pltpu.VMEM((tall, rows, width), low),
            pltpu.VMEM((tall, rows, width), low),
            pltpu.VMEM((tall, rows, width), low),
            pltpu.VMEM((tall, rows, width), low),
            pltpu.VMEM((n_h, 2, rows), wide),
            pltpu.SemaphoreType.DMA((8,)),
            pltpu.SemaphoreType.DMA((n_h,)),
            pltpu.SemaphoreType.DMA((n_h,)),
            pltpu.SemaphoreType.DMA((side,)),
            pltpu.SemaphoreType.DMA((side,)),
            pltpu.SemaphoreType.DMA((tall,)),
            pltpu.SemaphoreType.DMA((tall,)),
            pltpu.SemaphoreType.DMA((side,)),
            pltpu.SemaphoreType.DMA((side,)),
            pltpu.SemaphoreType.DMA((tall,)),
            pltpu.SemaphoreType.DMA((tall,)),
            pltpu.SemaphoreType.DMA((side,)),
            pltpu.SemaphoreType.DMA((side,)),
            pltpu.SemaphoreType.DMA((tall,)),
            pltpu.SemaphoreType.DMA((tall,)),
            pltpu.SemaphoreType.DMA((side,)),
            pltpu.SemaphoreType.DMA((side,)),
            pltpu.SemaphoreType.DMA((side,)),
            pltpu.SemaphoreType.DMA((side,)),
            pltpu.SemaphoreType.DMA((tall,)),
            pltpu.SemaphoreType.DMA((tall,)),
            pltpu.SemaphoreType.DMA((side,)),
            pltpu.SemaphoreType.DMA((side,)),
            pltpu.SemaphoreType.DMA((tall,)),
            pltpu.SemaphoreType.DMA((tall,)),
            pltpu.SemaphoreType.DMA((tall,)),
            pltpu.SemaphoreType.DMA((tall,)),
            pltpu.SemaphoreType.DMA((n_h,)),
            pltpu.SemaphoreType.DMA((n_h,)),
        ],
        compiler_params=pltpu.CompilerParams(
            collective_id=0, has_side_effects=True, vmem_limit_bytes=56 * 1024 * 1024
        ),
        cost_estimate=pl.CostEstimate(
            flops=10 * n_s * rows * rows * width,
            bytes_accessed=16 * rows * width,
            transcendentals=2 * n_s * rows * rows,
        ),
    )(
        *(
            pltpu.with_memory_space_constraint(array, pltpu.HBM)
            for array in (
                order,
                q_raw,
                k_raw,
                values,
                out,
                d_out,
                q_gain.reshape(1, width),
                k_gain.reshape(1, width),
            )
        )
    )
    return pl.pallas_call(
        deliver,
        out_shape=(block, block, block),
        in_specs=[vmem] * 3,
        out_specs=(hbm, hbm, hbm),
        scratch_shapes=[pltpu.SemaphoreType.DMA((3,))],
        compiler_params=pltpu.CompilerParams(vmem_limit_bytes=1024 * 1024),
    )(*(pltpu.with_memory_space_constraint(result, pltpu.VMEM) for result in results))


def solution(mesh):
    block = P("seq", "head")
    return jax.shard_map(
        functools.partial(local, mesh.shape["seq"], mesh.shape["head"]),
        mesh=mesh,
        in_specs=(block, block, block, block, block, P("head"), P("head"), P()),
        out_specs=(block, block, block),
        check_vma=False,
    )
```

```python
import functools
import math

import jax
import jax.numpy as jnp
from jax import lax
from jax.experimental import pallas as pl
from jax.experimental.pallas import tpu as pltpu
from jax.sharding import PartitionSpec as P

EPSILON = 1e-06
HIDDEN = -1e30
LOG2E = math.log2(math.e)
MESH = pl.DeviceIdType.MESH
NN = (((1,), (0,)), ((), ()))
NT = (((1,), (1,)), ((), ()))


def dot(a, b, dims):
    return lax.dot_general(a, b, dims, preferred_element_type=jnp.float32)


def each(low, high, body):
    if high - low <= 8:
        for j in range(low, high):
            body(j)
    else:

        def step(j, carry):
            body(j)
            return carry

        lax.fori_loop(low, high, step, 0)


def grid_of(n_s):
    root = math.isqrt(n_s)
    return (root, root) if root * root == n_s else (n_s, 1)


def kernel(
    n_s,
    n_h,
    order_hbm,
    q_hbm,
    k_hbm,
    v_hbm,
    o_hbm,
    do_hbm,
    qg_hbm,
    kg_hbm,
    d_q,
    d_k,
    d_v,
    order,
    q_raw,
    k_raw,
    out,
    d_out,
    q_gain,
    k_gain,
    x_t,
    q_scale,
    k_scale,
    qg_t,
    kg_t,
    keys,
    keys_t,
    queries,
    scores,
    dprobs,
    squares,
    q_in,
    k_in,
    q_rows,
    k_rows,
    grads,
    values,
    totals,
    q_moment,
    k_moment,
    dq_out,
    dq_in,
    dk_out,
    dk_in,
    dv_out,
    dv_in,
    inner,
    load,
    sq_send,
    sq_recv,
    qi_send,
    qi_recv,
    ki_send,
    ki_recv,
    qr_send,
    qr_recv,
    kr_send,
    kr_recv,
    gr_send,
    gr_recv,
    va_send,
    va_recv,
    to_send,
    to_recv,
    qm_send,
    qm_recv,
    km_send,
    km_recv,
    dq_send,
    dq_recv,
    dk_send,
    dk_recv,
    dv_send,
    dv_recv,
    inn_send,
    inn_recv,
):
    rows, width = q_raw.shape
    features = n_h * width
    root = width ** (-0.5)
    side, tall = grid_of(n_s)
    me = lax.axis_index("seq")
    mine = lax.axis_index("head")
    my_y, my_x = lax.div(me, side), lax.rem(me, side)

    def row_peer(step):
        return my_y * side + lax.rem(my_x + step, side)

    def column_peer(step):
        return lax.rem(my_y + step, tall) * side + my_x

    def head_peer(step):
        return lax.rem(mine + step, n_h)

    def remote(src, dst, send, recv, j, seq, head):
        return pltpu.make_async_remote_copy(
            src_ref=src,
            dst_ref=dst,
            send_sem=send.at[j],
            recv_sem=recv.at[j],
            device_id=(seq, head),
            device_id_type=MESH,
        )

    def to_row(buffer, send, recv):
        return lambda j: remote(
            buffer.at[0], buffer.at[j], send, recv, j, row_peer(j), mine
        )

    def to_column(buffer, send, recv):
        return lambda j: remote(
            buffer.at[0], buffer.at[j], send, recv, j, column_peer(j), mine
        )

    def to_heads(buffer, send, recv):
        return lambda j: remote(buffer.at[0], buffer.at[j], send, recv, j, me, head_peer(j))

    def back_row(source, target, send, recv):
        return lambda j: remote(
            source.at[j], target.at[j], send, recv, j, row_peer(side - j), mine
        )

    def back_column(source, target, send, recv):
        return lambda j: remote(
            source.at[j], target.at[j], send, recv, j, column_peer(tall - j), mine
        )

    barrier = pltpu.get_barrier_semaphore()

    def greet(seq, head):
        pl.semaphore_signal(barrier, inc=1, device_id=(seq, head), device_id_type=MESH)

    each(1, side, lambda j: greet(row_peer(j), mine))
    each(1, tall, lambda j: greet(column_peer(j), mine))
    each(1, n_h, lambda j: greet(me, head_peer(j)))

    loads = [
        pltpu.make_async_copy(src, dst, load.at[i])
        for i, (src, dst) in enumerate(
            (
                (q_hbm, q_raw),
                (k_hbm, k_raw),
                (do_hbm, d_out),
                (o_hbm, out),
                (qg_hbm, q_gain),
                (kg_hbm, k_gain),
                (v_hbm, values.at[0]),
                (order_hbm, order),
            )
        )
    ]
    for copy in loads:
        copy.start()

    squares_copy = to_heads(squares, sq_send, sq_recv)
    q_copy = to_row(q_in, qi_send, qi_recv)
    k_copy = to_column(k_in, ki_send, ki_recv)
    q_rows_copy = to_row(q_rows, qr_send, qr_recv)
    k_rows_copy = to_column(k_rows, kr_send, kr_recv)
    grads_copy = to_row(grads, gr_send, gr_recv)
    values_copy = to_column(values, va_send, va_recv)
    totals_copy = to_row(totals, to_send, to_recv)
    q_moment_copy = back_row(q_moment.at[0], q_moment.at[1], qm_send, qm_recv)
    k_moment_copy = back_column(k_moment.at[0], k_moment.at[1], km_send, km_recv)
    dq_copy = back_row(dq_out, dq_in, dq_send, dq_recv)
    dk_copy = back_column(dk_out, dk_in, dk_send, dk_recv)
    dv_copy = back_column(dv_out, dv_in, dv_send, dv_recv)
    inner_copy = to_heads(inner, inn_send, inn_recv)

    def alternate(along_row, along_column):
        @pl.when(lax.rem(mine, 2) == 0)
        def _():
            each(1, side, lambda j: along_row(j).start())
            each(1, tall, lambda j: along_column(j).start())

        @pl.when(lax.rem(mine, 2) == 1)
        def _():
            each(1, tall, lambda j: along_column(j).start())
            each(1, side, lambda j: along_row(j).start())

    loads[0].wait()
    x = q_raw[...].astype(jnp.float32).T
    x_t[...] = x
    q_in[0] = x.astype(jnp.bfloat16)
    squares[0, 0:1] = jnp.sum(x * x, axis=0, keepdims=True)
    loads[1].wait()
    y = k_raw[...].astype(jnp.float32).T
    k_in[0] = y.astype(jnp.bfloat16)
    squares[0, 1:2] = jnp.sum(y * y, axis=0, keepdims=True)

    pl.semaphore_wait(barrier, side + tall + n_h - 3)
    each(1, n_h, lambda j: squares_copy(j).start())
    alternate(q_copy, k_copy)

    loads[2].wait()
    loads[3].wait()
    grad = d_out[...].astype(jnp.float32)
    grads[0] = grad.T.astype(jnp.bfloat16)
    q_rows[0, 1:2] = jnp.sum((grad * out[...].astype(jnp.float32)).T, axis=0, keepdims=True)
    loads[4].wait()
    loads[5].wait()
    qg_t[...] = jnp.broadcast_to(q_gain[...].astype(jnp.float32), (rows, width)).T
    kg_t[...] = jnp.broadcast_to(k_gain[...].astype(jnp.float32), (rows, width)).T
    loads[6].wait()
    loads[7].wait()

    each(1, n_h, lambda j: squares_copy(j).wait_recv())
    rates = lax.rsqrt(jnp.sum(squares[...], axis=0) / features + EPSILON)
    q_rate, k_rate = rates[0:1], rates[1:2]
    q_rows[0, 0:1] = q_rate
    k_rows[0] = k_rate
    each(1, side, lambda j: q_rows_copy(j).start())
    each(1, tall, lambda j: k_rows_copy(j).start())
    alternate(grads_copy, values_copy)

    def form_query(j):
        query = q_in[j].astype(jnp.float32) * q_rows[j, 0:1] * qg_t[...]
        queries[j] = query.astype(jnp.bfloat16)

    def form_keys(j):
        key = k_in[j].astype(jnp.float32) * k_rows[j] * kg_t[...]
        keys_t[j] = key.astype(jnp.bfloat16)
        keys[j] = key.T.astype(jnp.bfloat16)

    row_total = [0.0] * side

    def seen(jx, jy):
        return order[row_peer(side - jx)] >= order[column_peer(tall - jy)]

    def score_tile(jx, jy):
        score = dot(keys[jy], queries[jx], NN) * (root * LOG2E)
        scores[jx, jy] = score
        total = jnp.sum(jnp.exp2(score), axis=0, keepdims=True)
        row_total[jx] += jnp.where(seen(jx, jy), total, 0.0)

    def dprob_tile(jx, jy):
        dprobs[jx, jy] = dot(values[jy], grads[jx], NN) - q_rows[jx, 1:2]

    form_query(0)
    form_keys(0)
    score_tile(0, 0)
    for jx in range(1, side):
        q_copy(jx).wait_recv()
        q_rows_copy(jx).wait_recv()
        form_query(jx)
        score_tile(jx, 0)
    for jy in range(1, tall):
        k_copy(jy).wait_recv()
        k_rows_copy(jy).wait_recv()
        form_keys(jy)
        for jx in range(side):
            score_tile(jx, jy)
    for jx in range(side):
        totals[0, lax.rem(my_x + side - jx, side)] = row_total[jx]
    each(1, side, lambda j: totals_copy(j).start())
    dprob_tile(0, 0)
    q_scale[...] = q_rate * qg_t[...]
    k_scale[...] = (k_rate * kg_t[...]).T
    for jx in range(1, side):
        grads_copy(jx).wait_recv()
        dprob_tile(jx, 0)
    for jy in range(1, tall):
        values_copy(jy).wait_recv()
        for jx in range(side):
            dprob_tile(jx, jy)
    each(1, side, lambda j: totals_copy(j).wait_recv())

    logs = [
        jnp.log2(sum(totals[i, lax.rem(my_x + side - jx, side)] for i in range(side)))
        for jx in range(side)
    ]
    ones = jnp.ones((16, rows), jnp.bfloat16)
    dq = [0.0] * side
    dk = [0.0] * tall
    dv = [0.0] * tall
    q_part = [0.0] * side
    k_part = [0.0] * tall

    def probs_of(jx, jy):
        return jnp.exp2(scores[jx, jy] - jnp.where(seen(jx, jy), logs[jx], -HIDDEN))

    def ds_of(jx, jy, probs):
        ds = probs * dprobs[jx, jy]
        moment = ds * scores[jx, jy]
        q_part[jx] += jnp.sum(moment, axis=0, keepdims=True)
        k_part[jy] += dot(ones, moment.astype(jnp.bfloat16), NT)[0:1]
        return ds.astype(jnp.bfloat16)

    probs, lows = {}, {}
    tiles = [(jx, jy) for jy in range(tall) for jx in range(side)][1:]
    for jx, jy in tiles:
        probs[jx, jy] = probs_of(jx, jy)
        lows[jx, jy] = ds_of(jx, jy, probs[jx, jy])
        probs[jx, jy] = probs[jx, jy].astype(jnp.bfloat16)
    for jy in range(1, tall):
        k_moment[0, jy] = k_part[jy]
        k_moment_copy(jy).start()
    for jx in range(1, side):
        q_moment[0, jx] = q_part[jx]
        q_moment_copy(jx).start()
    for jy in range(1, tall):
        for jx in range(side):
            dv[jy] += dot(probs[jx, jy], grads[jx], NT)
        dv_out[jy] = dv[jy].astype(jnp.bfloat16)
    for jx in range(1, side):
        for jy in range(tall):
            dq[jx] += dot(keys_t[jy], lows[jx, jy], NN)
        dq_out[jx] = (dq[jx] * root).astype(jnp.bfloat16)
    alternate(dq_copy, dv_copy)
    probs[0, 0] = probs_of(0, 0)
    lows[0, 0] = ds_of(0, 0, probs[0, 0])
    probs[0, 0] = probs[0, 0].astype(jnp.bfloat16)
    for jy in range(1, tall):
        for jx in range(side):
            dk[jy] += dot(lows[jx, jy], queries[jx], NT)
        dk_out[jy] = (dk[jy] * root).astype(jnp.bfloat16)

    q_inner, k_inner = q_part[0], k_part[0]
    for jy in range(1, tall):
        k_moment_copy(jy).wait_recv()
        k_inner = k_inner + k_moment[1, jy]
    for jx in range(1, side):
        q_moment_copy(jx).wait_recv()
        q_inner = q_inner + q_moment[1, jx]
    inner[0, 0:1] = q_inner
    inner[0, 1:2] = k_inner
    each(1, n_h, lambda j: inner_copy(j).start())
    each(1, tall, lambda j: dk_copy(j).start())

    for jy in range(tall):
        dq[0] += dot(keys_t[jy], lows[0, jy], NN)
    for jx in range(side):
        dk[0] += dot(lows[jx, 0], queries[jx], NT)
        dv[0] += dot(probs[jx, 0], grads[jx], NT)
    own_dv, own_dq, own_dk = dv[0], dq[0] * root, dk[0] * root
    for jy in range(1, tall):
        dv_copy(jy).wait_recv()
        own_dv = own_dv + dv_in[jy].astype(jnp.float32)
    d_v[...] = own_dv.astype(jnp.bfloat16)
    for jx in range(1, side):
        dq_copy(jx).wait_recv()
        own_dq = own_dq + dq_in[jx].astype(jnp.float32)
    grad_q = q_scale[...] * own_dq
    each(1, n_h, lambda j: inner_copy(j).wait_recv())
    products = jnp.sum(inner[...], axis=0) * (1.0 / (LOG2E * features))
    grad_q = grad_q - x_t[...] * (q_rate * q_rate * products[0:1])
    d_q[...] = grad_q.T.astype(jnp.bfloat16)
    pull = jnp.broadcast_to(k_rate * k_rate * products[1:2], (width, rows)).T
    for jy in range(1, tall):
        dk_copy(jy).wait_recv()
        own_dk = own_dk + dk_in[jy].astype(jnp.float32)
    d_k[...] = (k_scale[...] * own_dk - k_raw[...].astype(jnp.float32) * pull).astype(jnp.bfloat16)

    for copy in (squares_copy, inner_copy):
        each(1, n_h, lambda j: copy(j).wait_send())
    for copy in (q_copy, q_rows_copy, grads_copy, totals_copy, q_moment_copy, dq_copy):
        each(1, side, lambda j: copy(j).wait_send())
    for copy in (k_copy, k_rows_copy, values_copy, k_moment_copy, dk_copy, dv_copy):
        each(1, tall, lambda j: copy(j).wait_send())


def deliver(*refs):
    sems = refs[6]
    copies = [pltpu.make_async_copy(refs[i], refs[i + 3], sems.at[i]) for i in range(3)]
    for copy in copies:
        copy.start()
    for copy in copies:
        copy.wait()


def local(n_s, n_h, q_raw, k_raw, values, out, d_out, q_gain, k_gain, order):
    rows, width = q_raw.shape
    block = jax.ShapeDtypeStruct((rows, width), jnp.bfloat16)
    vmem = pl.BlockSpec(memory_space=pltpu.VMEM)
    hbm = pl.BlockSpec(memory_space=pltpu.HBM)
    low, wide = jnp.bfloat16, jnp.float32
    side, tall = grid_of(n_s)
    results = pl.pallas_call(
        functools.partial(kernel, n_s, n_h),
        out_shape=(block, block, block),
        in_specs=[hbm] * 8,
        out_specs=(vmem, vmem, vmem),
        scratch_shapes=[
            pltpu.SMEM((n_s,), jnp.int32),
            pltpu.VMEM((rows, width), low),
            pltpu.VMEM((rows, width), low),
            pltpu.VMEM((rows, width), low),
            pltpu.VMEM((rows, width), low),
            pltpu.VMEM((1, width), low),
            pltpu.VMEM((1, width), low),
            pltpu.VMEM((width, rows), wide),
            pltpu.VMEM((width, rows), wide),
            pltpu.VMEM((rows, width), wide),
            pltpu.VMEM((width, rows), wide),
            pltpu.VMEM((width, rows), wide),
            pltpu.VMEM((tall, rows, width), low),
            pltpu.VMEM((tall, width, rows), low),
            pltpu.VMEM((side, width, rows), low),
            pltpu.VMEM((side, tall, rows, rows), wide),
            pltpu.VMEM((side, tall, rows, rows), wide),
            pltpu.VMEM((n_h, 2, rows), wide),
            pltpu.VMEM((side, width, rows), low),
            pltpu.VMEM((tall, width, rows), low),
            pltpu.VMEM((side, 2, rows), wide),
            pltpu.VMEM((tall, 1, rows), wide),
            pltpu.VMEM((side, width, rows), low),
            pltpu.VMEM((tall, rows, width), low),
            pltpu.VMEM((side, side, 1, rows), wide),
            pltpu.VMEM((2, side, 1, rows), wide),
            pltpu.VMEM((2, tall, 1, rows), wide),
            pltpu.VMEM((side, width, rows), low),
            pltpu.VMEM((side, width, rows), low),
            pltpu.VMEM((tall, rows, width), low),
            pltpu.VMEM((tall, rows, width), low),
            pltpu.VMEM((tall, rows, width), low),
            pltpu.VMEM((tall, rows, width), low),
            pltpu.VMEM((n_h, 2, rows), wide),
            pltpu.SemaphoreType.DMA((8,)),
            pltpu.SemaphoreType.DMA((n_h,)),
            pltpu.SemaphoreType.DMA((n_h,)),
            pltpu.SemaphoreType.DMA((side,)),
            pltpu.SemaphoreType.DMA((side,)),
            pltpu.SemaphoreType.DMA((tall,)),
            pltpu.SemaphoreType.DMA((tall,)),
            pltpu.SemaphoreType.DMA((side,)),
            pltpu.SemaphoreType.DMA((side,)),
            pltpu.SemaphoreType.DMA((tall,)),
            pltpu.SemaphoreType.DMA((tall,)),
            pltpu.SemaphoreType.DMA((side,)),
            pltpu.SemaphoreType.DMA((side,)),
            pltpu.SemaphoreType.DMA((tall,)),
            pltpu.SemaphoreType.DMA((tall,)),
            pltpu.SemaphoreType.DMA((side,)),
            pltpu.SemaphoreType.DMA((side,)),
            pltpu.SemaphoreType.DMA((side,)),
            pltpu.SemaphoreType.DMA((side,)),
            pltpu.SemaphoreType.DMA((tall,)),
            pltpu.SemaphoreType.DMA((tall,)),
            pltpu.SemaphoreType.DMA((side,)),
            pltpu.SemaphoreType.DMA((side,)),
            pltpu.SemaphoreType.DMA((tall,)),
            pltpu.SemaphoreType.DMA((tall,)),
            pltpu.SemaphoreType.DMA((tall,)),
            pltpu.SemaphoreType.DMA((tall,)),
            pltpu.SemaphoreType.DMA((n_h,)),
            pltpu.SemaphoreType.DMA((n_h,)),
        ],
        compiler_params=pltpu.CompilerParams(
            collective_id=0, has_side_effects=True, vmem_limit_bytes=43 * 1024 * 1024
        ),
        cost_estimate=pl.CostEstimate(
            flops=10 * n_s * rows * rows * width,
            bytes_accessed=16 * rows * width,
            transcendentals=2 * n_s * rows * rows,
        ),
    )(
        *(
            pltpu.with_memory_space_constraint(array, pltpu.HBM)
            for array in (
                order,
                q_raw,
                k_raw,
                values,
                out,
                d_out,
                q_gain.reshape(1, width),
                k_gain.reshape(1, width),
            )
        )
    )
    return pl.pallas_call(
        deliver,
        out_shape=(block, block, block),
        in_specs=[vmem] * 3,
        out_specs=(hbm, hbm, hbm),
        scratch_shapes=[pltpu.SemaphoreType.DMA((3,))],
        compiler_params=pltpu.CompilerParams(vmem_limit_bytes=1024 * 1024),
    )(*(pltpu.with_memory_space_constraint(result, pltpu.VMEM) for result in results))


def solution(mesh):
    block = P("seq", "head")
    return jax.shard_map(
        functools.partial(local, mesh.shape["seq"], mesh.shape["head"]),
        mesh=mesh,
        in_specs=(block, block, block, block, block, P("head"), P("head"), P()),
        out_specs=(block, block, block),
        check_vma=False,
    )
```
